256 devices in a mesh: row: 32 (over y, x, core), col: 8 (over z).
Axes of the slice: x: 4, y: 4, z: 8, core: 2. Of those that a mesh axis runs over, the one named last changes fastest.
Arguments:
- tokens: bfloat16 [1024, 8192], P(None, 'row'), may hold values from -6 to 6
- gate_weight: bfloat16 [8192, 14336], P('row', 'col'), may hold values from -0.0625 to 0.0625
- up_weight: bfloat16 [8192, 14336], P('row', 'col'), may hold values from -0.0625 to 0.0625
- down_weight: bfloat16 [14336, 8192], P('col', 'row'), may hold values from -0.046875 to 0.046875
- cotangent: bfloat16 [1024, 8192], P(None, 'row'), may hold values from -6 to 6
Outputs:
- output: bfloat16 [1024, 8192], P(None, 'row')
- tokens_grad: bfloat16 [1024, 8192], P(None, 'row')
- gate_grad: bfloat16 [8192, 14336], P('row', 'col')
- up_grad: bfloat16 [8192, 14336], P('row', 'col')
- down_grad: bfloat16 [14336, 8192], P('col', 'row')
The draws below stay inside these ranges and needn't reach their ends.
All inputs are finite; a program needn't handle non-finite values.
Results may differ from the reference program's by a relative error of at most 0.035.
Values may be sent and summed in bfloat16 or wider, within the bound.
A program may use at most 64 MiB of HBM per device.

```python
import jax
import jax.numpy as jnp
from jax import lax

D = 8192
FF = 14336
TOKENS = 1024
N_ROW = 32


def raised(values, stream_key, source, target, blocks, factor):
    owner, partner = [(jnp.arange(values.shape[dim]) // (values.shape[dim] // blocks)).reshape([-1 if axis == dim else 1 for axis in range(values.ndim)]) for dim in (source, target)]
    chosen = jax.random.permutation(stream_key, blocks)[partner]
    strong = (owner == chosen) | (owner == (partner + blocks // 2) % blocks)
    return jnp.where(strong, factor * values, values)


def levels(rng, extent, pieces, least, top_value):
    level, own = 1.0, jax.random.fold_in(rng, 6)
    for axis_at, shards_of in pieces:
        heights = jnp.exp(jax.random.uniform(jax.random.fold_in(own, axis_at), (shards_of,), jnp.float32, least / len(pieces), top_value / len(pieces)))
        level = level * jnp.repeat(heights, extent[axis_at] // shards_of).reshape([-1 if axis == axis_at else 1 for axis in range(len(extent))])
    return level


def scatter_about(key, shape, scale, limit, pieces=(), kind=jnp.bfloat16):
    array = scale * jax.random.normal(key, shape, jnp.float32)
    if pieces:
        array = array * levels(key, shape, pieces, -0.22, 0.18)
    return jnp.clip(array, -limit, limit).astype(kind)


def bell_draw_with(rng, dims, spread, bound, pieces, heavy, kind=jnp.bfloat16):
    array = spread * jax.random.normal(rng, dims, jnp.float32)
    if pieces:
        array = array * levels(rng, dims, pieces, -0.22, 0.18)
    return jnp.clip(raised(array, jax.random.fold_in(rng, 3), *heavy), -bound, bound).astype(kind)


def setup_inputs(seed: int = 0) -> dict:
    seeds = jax.random.split(jax.random.key(seed), 6)
    tokens = bell_draw_with(seeds[0], (TOKENS, D), 1.0, 6.0, ((1, 32),), (1, 0, 32, 2.75))
    gate_weight = scatter_about(seeds[1], (D, FF), D ** -0.5, 0.0625, ((0, 32), (1, 8)))
    up_weight = scatter_about(seeds[2], (D, FF), D ** -0.5, 0.0625, ((0, 32), (1, 8)))
    down_weight = scatter_about(seeds[3], (FF, D), FF ** -0.5, 0.046875, ((0, 8), (1, 32)))
    cotangent = bell_draw_with(seeds[4], (TOKENS, D), 0.3, 6.0, ((1, 32),), (1, 0, 32, 2.75))
    return dict(tokens=tokens, gate_weight=gate_weight, up_weight=up_weight, down_weight=down_weight, cotangent=cotangent)


def blocked_sum(left, right, parts):
    width = left.shape[1] // parts

    def step(total, index):
        begin = (index * width).astype(jnp.int32)
        piece_left = lax.dynamic_slice_in_dim(left, begin, width, 1)
        piece_right = lax.dynamic_slice_in_dim(right, begin, width, 0)
        term = jnp.dot(piece_left, piece_right, preferred_element_type=jnp.float32)
        rounded = lax.optimization_barrier(term.astype(jnp.bfloat16))
        return total + rounded.astype(jnp.float32), None

    start = jnp.zeros((left.shape[0], right.shape[1]), jnp.float32)
    total, unused = lax.scan(step, start, jnp.arange(parts).astype(jnp.int32))
    return total.astype(jnp.bfloat16)


def reference(tokens, gate_weight, up_weight, down_weight, cotangent):
    gate = blocked_sum(tokens, gate_weight, N_ROW)
    up = blocked_sum(tokens, up_weight, N_ROW)
    gate_f = gate.astype(jnp.float32)
    up_f = up.astype(jnp.float32)
    sig = jax.nn.sigmoid(gate_f)
    hidden = (gate_f * sig * up_f).astype(jnp.bfloat16)
    output = jnp.dot(hidden, down_weight, preferred_element_type=jnp.float32).astype(jnp.bfloat16)
    down_grad = jnp.dot(hidden.T, cotangent, preferred_element_type=jnp.float32).astype(jnp.bfloat16)
    hidden_grad = blocked_sum(cotangent, down_weight.T, N_ROW).astype(jnp.float32)
    gate_pre = (hidden_grad * up_f * sig * (1.0 + gate_f * (1.0 - sig))).astype(jnp.bfloat16)
    up_pre = (hidden_grad * gate_f * sig).astype(jnp.bfloat16)
    gate_grad = jnp.dot(tokens.T, gate_pre, preferred_element_type=jnp.float32).astype(jnp.bfloat16)
    up_grad = jnp.dot(tokens.T, up_pre, preferred_element_type=jnp.float32).astype(jnp.bfloat16)
    tokens_grad = (jnp.dot(gate_pre, gate_weight.T, preferred_element_type=jnp.float32)
                   + jnp.dot(up_pre, up_weight.T, preferred_element_type=jnp.float32)).astype(jnp.bfloat16)
    return output, tokens_grad, gate_grad, up_grad, down_grad
```

```python
import functools

import jax
import jax.numpy as jnp
from jax import lax
from jax.experimental import pallas as pl
from jax.experimental.pallas import tpu as pltpu
from jax.sharding import PartitionSpec as P

MESH = pl.DeviceIdType.MESH
BF, F32 = jnp.bfloat16, jnp.float32
CHUNKS, RING, ROWS, N_Z = 4, 4, 16, 8
BLOCK = RING * RING * ROWS
WIDTH, HALF = 256, 896
COLS = 3 * HALF
SPLIT = 1408
N_SEMS = 48

ORDER = [
    (0, 0), (0, 1), (1, 0), (2, 0), (1, 1), (3, 0), (0, 2), (4, 0), (2, 1), (5, 0), (3, 1), (1, 2), (6, 0),
    (4, 1), (0, 3), (2, 2), (5, 1), (7, 0), (3, 2), (6, 1), (1, 3), (8, 0), (4, 2), (2, 3), (5, 2), (7, 1),
    (3, 3), (9, 0), (6, 2), (8, 1), (4, 3), (10, 0), (5, 3), (7, 2), (9, 1), (6, 3), (11, 0), (8, 2), (10, 1), (7, 3), (9, 2),
    (11, 1), (8, 3), (10, 2), (9, 3),
]


def dot(left, right):
    return jnp.dot(left, right, preferred_element_type=F32)


def dot_t(left, right):
    return lax.dot_general(left, right, (((1,), (1,)), ((), ())), preferred_element_type=F32)


def kernel(
    tok_in, gw_in, uw_in, dw_in, cot_in,
    out, tok_grad, gate_grad, up_grad, down_grad,
    tok, cot, tok_p, cot_p, gu, gu_p, dw, dw_p, tok_t, cot_t,
    part, rec_a, rec_b, rec_l, rec_r, summed, sec_a, sec_b, sec_l, sec_r,
    own, other, z_part, z_rec, z_sum, grads, grads_d,
    send, recv, swap_send, swap_recv, local,
):
    row, z = lax.axis_index("row"), lax.axis_index("col")
    y, x, core = row // 8, (row // 2) % 4, row % 2
    a = x + core * (y - x)
    b = y + core * (x - y)

    def step_a(by):
        return (
            ((y + core * by + 4) % 4) * 8 + ((x + (1 - core) * by + 4) % 4) * 2 + core,
            z,
        )

    def step_b(by):
        return (
            ((y + (1 - core) * by + 4) % 4) * 8 + ((x + core * by + 4) % 4) * 2 + core,
            z,
        )

    a_next, a_prev, b_next, b_prev = step_a(1), step_a(-1), step_b(1), step_b(-1)
    partner = (y * 8 + x * 2 + 1 - core, z)
    others = [(row, (z + j) % N_Z) for j in range(1, N_Z)]
    a1, a2, a3 = (a + 1) % 4, (a + 2) % 4, (a + 3) % 4
    b1, b2, b3 = (b + 1) % 4, (b + 2) % 4, (b + 3) % 4
    left, right = pl.ds(0, SPLIT), pl.ds(SPLIT, COLS - SPLIT)
    mine = pl.multiple_of(core * HALF, 128)
    theirs = pl.multiple_of((1 - core) * HALF, 128)

    loads = [
        (gw_in.at[:, pl.ds(h * HALF, HALF)], gu.at[h, :, pl.ds(0, HALF)]) for h in range(2)
    ] + [
        (uw_in.at[:, pl.ds(h * HALF, HALF)], gu.at[h, :, pl.ds(HALF, HALF)]) for h in range(2)
    ] + [(dw_in, dw)]
    loads = [pltpu.make_async_copy(s, d, local.at[i]) for i, (s, d) in enumerate(loads)]

    @pl.when(core == 0)
    def _():
        pltpu.make_async_copy(tok_in, tok, local.at[5]).start()
        pltpu.make_async_copy(cot_in, cot, local.at[6]).start()

    @pl.when(core == 1)
    def _():
        for k in range(4):
            pltpu.make_async_copy(tok_in.at[:, :, k], tok.at[:, k], local.at[5]).start()
        for k in range(4):
            pltpu.make_async_copy(cot_in.at[:, :, k], cot.at[:, k], local.at[6]).start()

    for load in loads:
        load.start()

    barrier = pltpu.get_barrier_semaphore()
    peers = [partner, a_next, a_prev, b_next, b_prev] + others
    for peer in peers:
        pl.semaphore_signal(barrier, inc=1, device_id=peer, device_id_type=MESH)
    pl.semaphore_wait(barrier, len(peers))

    def remote(src, dst, s, r, to):
        return pltpu.make_async_remote_copy(
            src_ref=src, dst_ref=dst, send_sem=s, recv_sem=r, device_id=to, device_id_type=MESH
        )

    def swap(src, dst, i):
        return remote(src, dst, swap_send.at[i], swap_recv.at[i], partner)

    swaps = [
        swap(tok_in, tok_p, 0),
        swap(gw_in.at[:, pl.ds(theirs, HALF)], gu_p.at[:, pl.ds(0, HALF)], 1),
        swap(uw_in.at[:, pl.ds(theirs, HALF)], gu_p.at[:, pl.ds(HALF, HALF)], 2),
        swap(cot_in, cot_p, 3),
        swap(dw_in.at[1 - core], dw_p, 4),
    ]

    def swap_rows(src, dst, i):
        @pl.when(core == 1)
        def _():
            swap(src, dst, i).start()

        @pl.when(core == 0)
        def _():
            for k in range(4):
                swap(src.at[:, :, k], dst.at[:, k], i).start()

    swap_rows(tok_in, tok_p, 0)
    swaps[1].start()
    swaps[2].start()
    swap_rows(cot_in, cot_p, 3)
    swaps[4].start()

    pltpu.make_async_copy(tok_in, tok, local.at[5]).wait()
    pltpu.make_async_copy(cot_in, cot, local.at[6]).wait()
    for load in loads:
        load.wait()

    sent = []
    flows = {}

    def start(r, name, src, dst, to):
        i = len([key for key in flows if key[0] == r])
        copy = remote(src, dst, send.at[r, i], recv.at[r, i], to)
        flows[r, name] = copy
        copy.start()

    def arrived(r, *names):
        for name in names:
            flows[r, name].wait_recv()

    def flat(value):
        return value.reshape((BLOCK, value.shape[-1]))

    def project(r):
        t, tp = flat(tok[r]), flat(tok_p[r])
        for n in range(7):
            cols = pl.ds(n * 256, 256)
            total = dot(t, gu[core, :, cols]) + dot(tp, gu_p[:, cols])
            part[r, :, :, :, cols] = total.astype(BF).reshape((RING, RING, ROWS, 256))
        c, cp = flat(cot[r]), flat(cot_p[r])
        for n in range(0, HALF, 256):
            size = min(256, HALF - n)
            units = pl.ds(n, size)
            total = dot_t(c, dw[core, units, :]) + dot_t(cp, dw_p[units, :])
            part[r, :, :, :, pl.ds(2 * HALF + n, size)] = total.astype(BF).reshape((RING, RING, ROWS, size))

    def add(blocks, into, terms, begin, size):
        def step(i, carry):
            for n in range(begin, begin + size, 640 if size % 640 == 0 else 128 * 11 if size == SPLIT else 896):
                width = 640 if size % 640 == 0 else 128 * 11 if size == SPLIT else 896
                cols = pl.ds(n, width)
                total = terms[0](i, cols).astype(F32)
                for term in terms[1:]:
                    total = total + term(i, cols).astype(F32)
                into(i, cols, total.astype(BF))
            return carry

        lax.fori_loop(0, blocks, step, 0)

    def stage0(r):
        if r == 0:
            for copy in swaps:
                copy.wait_recv()
        project(r)
        start(r, "a1+", part.at[r, a2, :, :, left], rec_a.at[r], a_next)
        start(r, "a1-", part.at[r, a2, :, :, right], rec_b.at[r], a_prev)
        start(r, "a2+R", part.at[r, a1, :, :, right], rec_l.at[r, :, :, right], a_next)
        start(r, "a2-L", part.at[r, a3, :, :, left], rec_r.at[r, :, :, left], a_prev)

    def put_part(r, k):
        def put(i, cols, value):
            part[r, k, i, :, cols] = value
        return put

    def stage1(r):
        arrived(r, "a1+", "a1-")
        add(4, put_part(r, a1), [lambda i, cols: part[r, a1, i, :, cols], lambda i, cols: rec_a[r, i, :, cols]], 0, SPLIT)
        start(r, "a2+L", part.at[r, a1, :, :, left], rec_l.at[r, :, :, left], a_next)
        add(
            4, put_part(r, a3),
            [
                lambda i, cols: part[r, a3, i, :, cols],
                lambda i, cols: rec_b[r, i, :, pl.ds(cols.start - SPLIT, cols.size)],
            ],
            SPLIT, COLS - SPLIT,
        )
        start(r, "a2-R", part.at[r, a3, :, :, right], rec_r.at[r, :, :, right], a_prev)

    def stage2(r):
        arrived(r, "a2+R", "a2-L", "a2+L", "a2-R")

        def put(i, cols, value):
            summed[r, i, :, cols] = value

        add(
            4, put,
            [
                lambda i, cols: part[r, a, i, :, cols],
                lambda i, cols: rec_l[r, i, :, cols],
                lambda i, cols: rec_r[r, i, :, cols],
            ],
            0, COLS,
        )
        start(r, "b1+", summed.at[r, b2, :, left], sec_a.at[r], b_next)
        start(r, "b1-", summed.at[r, b2, :, right], sec_b.at[r], b_prev)
        start(r, "b2+R", summed.at[r, b1, :, right], sec_l.at[r, :, right], b_next)
        start(r, "b2-L", summed.at[r, b3, :, left], sec_r.at[r, :, left], b_prev)

    def stage3(r):
        arrived(r, "b1+", "b1-")
        value = summed[r, b1, :, left].astype(F32) + sec_a[r].astype(F32)
        summed[r, b1, :, left] = value.astype(BF)
        start(r, "b2+L", summed.at[r, b1, :, left], sec_l.at[r, :, left], b_next)
        value = summed[r, b3, :, right].astype(F32) + sec_b[r].astype(F32)
        summed[r, b3, :, right] = value.astype(BF)
        start(r, "b2-R", summed.at[r, b3, :, right], sec_r.at[r, :, right], b_prev)

    def stage4(r):
        arrived(r, "b2+R", "b2-L", "b2+L", "b2-R")

        def total(k):
            cols = pl.ds(k * HALF, HALF)
            value = summed[r, b, :, cols].astype(F32) + sec_l[r, :, cols].astype(F32) + sec_r[r, :, cols].astype(F32)
            return value.astype(BF).astype(F32)

        gate, up, grad = total(0), total(1), total(2)
        sig = jax.nn.sigmoid(gate)
        own[r, a, b, :, pl.ds(0, HALF)] = (gate * sig * up).astype(BF)
        own[r, a, b, :, pl.ds(HALF, HALF)] = (grad * up * sig * (1.0 + gate * (1.0 - sig))).astype(BF)
        own[r, a, b, :, pl.ds(2 * HALF, HALF)] = (grad * gate * sig).astype(BF)
        start(r, "c1+", own.at[r, a, b], own.at[r, a, b], b_next)
        start(r, "c1-", own.at[r, a, b], own.at[r, a, b], b_prev)

    def stage5(r):
        arrived(r, "c1+", "c1-")
        start(r, "c2+", own.at[r, a, b3, :, left], own.at[r, a, b3, :, left], b_next)
        start(r, "c2-", own.at[r, a, b1, :, right], own.at[r, a, b1, :, right], b_prev)

    def share(r, name, k):
        start(r, name, own.at[r, k], other.at[r, :, k], partner)

    def stage6(r):
        arrived(r, "c2+", "c2-")
        start(r, "d1+", own.at[r, a], own.at[r, a], a_next)
        start(r, "d1-", own.at[r, a], own.at[r, a], a_prev)
        share(r, "s0", a)

    def stage7(r):
        arrived(r, "d1+", "d1-")
        start(r, "d2+", own.at[r, a3, :, :, left], own.at[r, a3, :, :, left], a_next)
        start(r, "d2-", own.at[r, a1, :, :, right], own.at[r, a1, :, :, right], a_prev)
        share(r, "s1", a1)
        share(r, "s3", a3)

    def stage8(r):
        arrived(r, "d2+", "d2-")
        share(r, "s2", a2)

    def stage9(r):
        arrived(r, "s0", "s1", "s3", "s2")
        hidden, pre = pl.ds(0, HALF), pl.ds(HALF, 2 * HALF)
        total = dot(flat(own[r, :, :, :, hidden]), dw[core]) + dot(flat(other[r, :, :, :, hidden]), dw[1 - core])
        z_part[r, :, :, pl.ds(0, WIDTH)] = total.astype(BF).reshape((RING * RING, ROWS, WIDTH))
        total = dot_t(flat(own[r, :, :, :, pre]), gu[core]) + dot_t(flat(other[r, :, :, :, pre]), gu[1 - core])
        z_part[r, :, :, pl.ds(WIDTH, WIDTH)] = total.astype(BF).reshape((RING * RING, ROWS, WIDTH))
        for j in (4, 3, 5, 2, 6, 1, 7):
            target = (z + j) % N_Z
            start(r, f"e{j}", z_part.at[r, pl.ds(target * 2, 2)], z_rec.at[r, j - 1], others[j - 1])

    def stage10(r):
        arrived(r, *[f"e{j}" for j in range(1, N_Z)])
        total = z_part[r, pl.ds(z * 2, 2)].astype(F32)
        for j in range(N_Z - 1):
            total = total + z_rec[r, j].astype(F32)
        here = z_sum.at[r, pl.ds(z * 2, 2)]
        z_sum[r, pl.ds(z * 2, 2)] = total.astype(BF)
        for j in (4, 3, 5, 2, 6, 1, 7):
            start(r, f"f{j}", here, here, others[j - 1])

    def stores(r):
        result = []
        for k in range(4):
            for n, array in enumerate((out, tok_grad)):
                result.append((k, n, array))
        return result

    def stage11(r):
        arrived(r, *[f"f{j}" for j in range(1, N_Z)])

        @pl.when(core == 0)
        def _():
            for k in range(4):
                for n, array in enumerate((out, tok_grad)):
                    pltpu.make_async_copy(
                        z_sum.at[r, pl.ds(4 * k, 4), :, pl.ds(n * WIDTH, WIDTH)], array.at[r, k], local.at[7 + n]
                    ).start()

        @pl.when(core == 1)
        def _():
            for k in range(4):
                for n, array in enumerate((out, tok_grad)):
                    pltpu.make_async_copy(
                        z_sum.at[r, pl.ds(4 * k, 4), :, pl.ds(n * WIDTH, WIDTH)], array.at[r, :, k], local.at[7 + n]
                    ).start()

    def weight_grads(k, half, held):
        t, c = tok_t[...], cot_t[...]

        def tall(cols):
            return held[:, :, :, :, cols].reshape((CHUNKS * BLOCK, cols.size))

        for n in range(7):
            grads[k, :, pl.ds(n * 256, 256)] = dot(t, tall(pl.ds(HALF + n * 256, 256))).astype(BF)
        for n in range(0, HALF, 256):
            size = min(256, HALF - n)
            grads_d[k, pl.ds(n, size), :] = dot(c, tall(pl.ds(n, size))).T.astype(BF)
        cols = pl.ds(pl.multiple_of(half * HALF, 128), HALF)
        copies = [
            pltpu.make_async_copy(grads.at[k, :, pl.ds(0, HALF)], gate_grad.at[:, cols], local.at[9 + 3 * k]),
            pltpu.make_async_copy(grads.at[k, :, pl.ds(HALF, HALF)], up_grad.at[:, cols], local.at[10 + 3 * k]),
            pltpu.make_async_copy(grads_d.at[k], down_grad.at[half], local.at[11 + 3 * k]),
        ]
        for copy in copies:
            copy.start()
        return copies

    stages = [
        stage0, stage1, stage2, stage3, stage4, stage5, stage6, stage7, stage8, stage9, stage10, stage11,
    ]
    for i, (stage, r) in enumerate(ORDER):
        stages[stage](r)
        if i == 2:
            tok_t[...] = tok[...].reshape((CHUNKS * BLOCK, WIDTH)).T
            cot_t[...] = cot[...].reshape((CHUNKS * BLOCK, WIDTH)).T
    copies = weight_grads(0, core, own)
    stage10(3)
    copies += weight_grads(1, 1 - core, other)
    stage11(2)
    stage11(3)
    for copy in swaps:
        copy.wait_send()
    for copy in flows.values():
        copy.wait_send()
    pltpu.make_async_copy(out, out, local.at[7]).wait()
    pltpu.make_async_copy(tok_grad, tok_grad, local.at[8]).wait()
    for copy in copies:
        copy.wait()


def per_device(tokens, gate_weight, up_weight, down_weight, cotangent):
    rows = (CHUNKS, RING, RING, ROWS, WIDTH)
    grad = (CHUNKS, RING, RING, ROWS)
    V = pltpu.VMEM
    wide = (CHUNKS, RING, ROWS, COLS)
    any_space = pl.BlockSpec(memory_space=pl.ANY)
    S = jax.ShapeDtypeStruct
    outs = pl.pallas_call(
        kernel,
        out_shape=(
            S(rows, BF), S(rows, BF), S((WIDTH, 2 * HALF), BF), S((WIDTH, 2 * HALF), BF), S((2, HALF, WIDTH), BF),
        ),
        in_specs=[any_space] * 5,
        out_specs=[any_space] * 5,
        scratch_shapes=[
            V(rows, BF), V(rows, BF), V(rows, BF), V(rows, BF),
            V((2, WIDTH, 2 * HALF), BF), V((WIDTH, 2 * HALF), BF),
            V((2, HALF, WIDTH), BF), V((HALF, WIDTH), BF),
            V((WIDTH, CHUNKS * BLOCK), BF), V((WIDTH, CHUNKS * BLOCK), BF),
            V(grad + (COLS,), BF),
            V((CHUNKS, RING, ROWS, SPLIT), BF), V((CHUNKS, RING, ROWS, COLS - SPLIT), BF),
            V(wide, BF), V(wide, BF), V(wide, BF),
            V((CHUNKS, ROWS, SPLIT), BF), V((CHUNKS, ROWS, COLS - SPLIT), BF),
            V((CHUNKS, ROWS, COLS), BF), V((CHUNKS, ROWS, COLS), BF),
            V(grad + (COLS,), BF), V(grad + (COLS,), BF),
            V((CHUNKS, RING * RING, ROWS, 2 * WIDTH), BF),
            V((CHUNKS, N_Z - 1, 2, ROWS, 2 * WIDTH), BF),
            V((CHUNKS, RING * RING, ROWS, 2 * WIDTH), BF),
            V((2, WIDTH, 2 * HALF), BF), V((2, HALF, WIDTH), BF),
            pltpu.SemaphoreType.DMA((CHUNKS, N_SEMS)), pltpu.SemaphoreType.DMA((CHUNKS, N_SEMS)),
            pltpu.SemaphoreType.DMA((5,)), pltpu.SemaphoreType.DMA((5,)),
            pltpu.SemaphoreType.DMA((15,)),
        ],
        compiler_params=pltpu.CompilerParams(
            collective_id=0, has_side_effects=True, vmem_limit_bytes=58 << 20
        ),
    )(
        tokens.reshape(rows), gate_weight, up_weight, down_weight.reshape((2, HALF, WIDTH)), cotangent.reshape(rows),
    )
    output, tokens_grad, gate_grad, up_grad, down_grad = outs
    return (
        output.reshape(tokens.shape), tokens_grad.reshape(tokens.shape), gate_grad, up_grad,
        down_grad.reshape(down_weight.shape),
    )


def solution(mesh):
    return jax.shard_map(
        per_device,
        mesh=mesh,
        in_specs=(
            P(None, "row"),
            P("row", "col"),
            P("row", "col"),
            P("col", "row"),
            P(None, "row"),
        ),
        out_specs=(
            P(None, "row"),
            P(None, "row"),
            P("row", "col"),
            P("row", "col"),
            P("col", "row"),
        ),
        check_vma=False,
    )
```

```python
import functools

import jax
import jax.numpy as jnp
from jax import lax
from jax.experimental import pallas as pl
from jax.experimental.pallas import tpu as pltpu
from jax.sharding import PartitionSpec as P

MESH = pl.DeviceIdType.MESH
BF, F32 = jnp.bfloat16, jnp.float32
CHUNKS, RING, ROWS, N_Z = 4, 4, 16, 8
BLOCK = RING * RING * ROWS
WIDTH, HALF = 256, 896
N_SEMS = 40
TREE = {(0, 1), (2, 1), (0, 0), (1, 1), (2, 0), (3, 0), (1, 0)}
Z_PEERS = (1, 2, 3, 4, 5, 6, 7)
RS_LEFT, RS_RIGHT = (pl.ds(0, 896), pl.ds(0, 512)), (pl.ds(896, 896), pl.ds(512, 384))
AG_LEFT, AG_RIGHT = (pl.ds(0, 512), pl.ds(0, 896)), (pl.ds(512, 384), pl.ds(896, 896))

ORDER = [
    (0, 0, 0), (0, 0, 1), (14, 0, 0), (0, 1, 0), (1, 0, 0), (1, 0, 1), (0, 1, 1), (1, 1, 0),
    (0, 2, 0), (2, 0, 0), (2, 0, 1), (1, 1, 1), (2, 1, 0), (0, 2, 1), (1, 2, 0), (3, 0, 0),
    (3, 0, 1), (0, 3, 0), (3, 1, 0), (2, 1, 1), (1, 2, 1), (2, 2, 0), (4, 0, 0), (4, 0, 1),
    (1, 3, 0), (4, 1, 0), (3, 1, 1), (0, 3, 1), (2, 2, 1), (3, 2, 0), (5, 0, 0), (5, 0, 1),
    (2, 3, 0), (5, 1, 0), (4, 1, 1), (1, 3, 1), (3, 2, 1), (4, 2, 0), (6, 0, 0), (6, 0, 1),
    (3, 3, 0), (6, 1, 0), (5, 1, 1), (2, 3, 1), (4, 2, 1), (5, 2, 0), (7, 0, 0), (7, 0, 1),
    (4, 3, 0), (7, 1, 0), (6, 1, 1), (3, 3, 1), (5, 2, 1), (6, 2, 0), (8, 0, 0), (8, 0, 1),
    (9, 0, 0), (5, 3, 0), (8, 1, 0), (9, 0, 1), (9, 1, 0), (7, 1, 1), (4, 3, 1), (15, 0, 0),
    (6, 2, 1), (7, 2, 0), (15, 0, 1), (6, 3, 0), (15, 1, 0), (8, 1, 1), (10, 0, 0), (5, 3, 1),
    (9, 1, 1), (10, 0, 1), (10, 1, 0), (7, 2, 1), (8, 2, 0), (16, 0, 0), (7, 3, 0), (9, 2, 0),
    (6, 3, 1), (15, 1, 1), (16, 0, 1), (8, 2, 1), (16, 1, 0), (8, 3, 0), (9, 2, 1), (11, 0, 0),
    (9, 3, 0), (15, 2, 0), (12, 0, 0), (7, 3, 1), (10, 1, 1), (11, 0, 1), (11, 1, 0), (12, 1, 0),
    (15, 2, 1), (15, 3, 0), (8, 3, 1), (10, 2, 0), (16, 1, 1), (9, 3, 1), (10, 2, 1), (13, 0, 1),
    (10, 3, 0), (16, 2, 0), (11, 1, 1), (13, 1, 1), (10, 3, 1), (16, 2, 1), (16, 3, 0), (11, 2, 0),
    (11, 3, 1), (11, 2, 1), (11, 3, 0),]


def dot(left, right):
    return jnp.dot(left, right, preferred_element_type=F32)


def dot_t(left, right):
    return lax.dot_general(left, right, (((1,), (1,)), ((), ())), preferred_element_type=F32)


def kernel(
    tok_in, gw_in, uw_in, dw_in, cot_in,
    z_sum, grads, grads_d,
    tok, cot, tok_p, cot_p, gu, gu_p, dw, dw_p, tok_t, cot_t,
    part, rec_a, rec_b, rec_l, rec_r, summed, sec_a, sec_b, sec_l, sec_r,
    acts, own, other, z_part, z_rec,
    send, recv, swap_send, swap_recv, local,
):
    row, z = lax.axis_index("row"), lax.axis_index("col")
    y, x, core = row // 8, (row // 2) % 4, row % 2
    a = x + core * (y - x)
    b = y + core * (x - y)

    def step_a(by):
        return (
            ((y + core * by + 4) % 4) * 8 + ((x + (1 - core) * by + 4) % 4) * 2 + core,
            z,
        )

    def step_b(by):
        return (
            ((y + (1 - core) * by + 4) % 4) * 8 + ((x + core * by + 4) % 4) * 2 + core,
            z,
        )

    a_next, a_prev, b_next, b_prev = step_a(1), step_a(-1), step_b(1), step_b(-1)
    partner = (y * 8 + x * 2 + 1 - core, z)
    others = [(row, (z + j) % N_Z) for j in range(1, N_Z)]
    a1, a2, a3 = (a + 1) % 4, (a + 2) % 4, (a + 3) % 4
    b1, b2, b3 = (b + 1) % 4, (b + 2) % 4, (b + 3) % 4
    theirs = pl.multiple_of((1 - core) * HALF, 128)

    waits = {}

    def rows_of(ref, first, count):
        return ref.at[pl.ds(first, count)]

    def load(name, src, dst):
        i = len(waits)
        copy = pltpu.make_async_copy(src, dst, local.at[i])
        waits[name] = copy.wait
        copy.start()

    def load_rows(name, src, dst, first, count):
        sem = local.at[len(waits)]
        waits[name] = pltpu.make_async_copy(rows_of(src, first, count), rows_of(dst, first, count), sem).wait

        @pl.when(core == 0)
        def _():
            pltpu.make_async_copy(rows_of(src, first, count), rows_of(dst, first, count), sem).start()

        @pl.when(core == 1)
        def _():
            for k in range(4):
                pltpu.make_async_copy(
                    src.at[pl.ds(first, count), :, k], dst.at[pl.ds(first, count), k], sem
                ).start()

    def use(*names):
        for name in names:
            if name in waits:
                waits.pop(name)()

    def load_weights(name, half):
        cols = pl.ds(pl.multiple_of(half * HALF, 128), HALF)
        load(name + "_gate", gw_in.at[:, cols], gu.at[half, :, pl.ds(0, HALF)])
        load(name + "_up", uw_in.at[:, cols], gu.at[half, :, pl.ds(HALF, HALF)])
        load(name + "_down", dw_in.at[half], dw.at[half])

    load_rows("tok0", tok_in, tok, 0, 1)
    load_weights("mine", core)
    load_rows("cot0", cot_in, cot, 0, 1)

    barrier = pltpu.get_barrier_semaphore()
    peers = [partner, a_next, a_prev, b_next, b_prev] + [others[j - 1] for j in Z_PEERS]
    for peer in peers:
        pl.semaphore_signal(barrier, inc=1, device_id=peer, device_id_type=MESH)
    pl.semaphore_wait(barrier, len(peers))

    def remote(src, dst, s, r, to):
        return pltpu.make_async_remote_copy(
            src_ref=src, dst_ref=dst, send_sem=s, recv_sem=r, device_id=to, device_id_type=MESH
        )

    swaps = []

    def swap(name, src, dst):
        copy = remote(src, dst, swap_send.at[len(swaps)], swap_recv.at[len(swaps)], partner)
        swaps.append(copy)
        waits[name] = copy.wait_recv
        copy.start()

    def swap_rows(name, src, dst, first, count):
        i = len(swaps)

        def part_copy(src, dst):
            return remote(src, dst, swap_send.at[i], swap_recv.at[i], partner)

        whole = part_copy(rows_of(src, first, count), rows_of(dst, first, count))
        swaps.append(whole)
        waits[name] = whole.wait_recv

        @pl.when(core == 1)
        def _():
            whole.start()

        @pl.when(core == 0)
        def _():
            for k in range(4):
                part_copy(src.at[pl.ds(first, count), :, k], dst.at[pl.ds(first, count), k]).start()

    swap_rows("tok_p0", tok_in, tok_p, 0, 1)
    swap("gate_p", gw_in.at[:, pl.ds(theirs, HALF)], gu_p.at[:, pl.ds(0, HALF)])
    swap("up_p", uw_in.at[:, pl.ds(theirs, HALF)], gu_p.at[:, pl.ds(HALF, HALF)])
    swap_rows("cot_p0", cot_in, cot_p, 0, 1)
    swap("down_p", dw_in.at[1 - core], dw_p)
    swap_rows("tok_p1", tok_in, tok_p, 1, CHUNKS - 1)
    swap_rows("cot_p1", cot_in, cot_p, 1, CHUNKS - 1)
    load_rows("tok1", tok_in, tok, 1, CHUNKS - 1)
    load_rows("cot1", cot_in, cot, 1, CHUNKS - 1)
    load_weights("theirs", 1 - core)

    flows = {}

    def start(unit, name, src, dst, to):
        r, g = unit
        i = len([key for key in flows if key[0] == unit])
        copy = remote(src, dst, send.at[2 * r + g, i], recv.at[2 * r + g, i], to)
        flows[unit, name] = copy
        copy.start()

    def arrived(unit, *names):
        for name in names:
            flows[unit, name].wait_recv()

    def flat(value):
        return value.reshape((BLOCK, value.shape[-1]))

    def add(blocks, begin, size, into, *terms):
        width = min(size, HALF)

        def step(i, carry):
            for n in range(begin, begin + size, width):
                total = terms[0](i, n, width).astype(F32)
                for term in terms[1:]:
                    total = total + term(i, n, width).astype(F32)
                into(i, n, width, total.astype(BF))
            return carry

        lax.fori_loop(0, blocks, step, 0)

    def stage0(unit):
        r, g = unit
        late = "" if r == 0 else "1"
        if g == 0:
            use("tok0", "mine_gate", "mine_up", "tok_p0", "gate_p", "up_p", "tok" + late, "tok_p" + late)
        else:
            use("cot0", "mine_down", "cot_p0", "down_p", "cot" + late, "cot_p" + late)
        dst = part[g]
        if g == 0:
            t, tp = flat(tok[r]), flat(tok_p[r])
            for n in range(0, 2 * HALF, 256):
                cols = pl.ds(n, 256)
                total = dot(t, gu[core, :, cols]) + dot(tp, gu_p[:, cols])
                dst[r, :, :, :, cols] = total.astype(BF).reshape((RING, RING, ROWS, 256))
        else:
            c, cp = flat(cot[r]), flat(cot_p[r])
            for n in range(0, HALF, 256):
                size = min(256, HALF - n)
                units = pl.ds(n, size)
                total = dot_t(c, dw[core, units, :]) + dot_t(cp, dw_p[units, :])
                dst[r, :, :, :, units] = total.astype(BF).reshape((RING, RING, ROWS, size))
        left, right = RS_LEFT[g], RS_RIGHT[g]
        start(unit, "a1+", dst.at[r, a2, :, :, left], rec_a[g].at[r], a_next)
        start(unit, "a1-", dst.at[r, a2, :, :, right], rec_b[g].at[r], a_prev)
        start(unit, "a2+R", dst.at[r, a1, :, :, right], rec_l[g].at[r, :, :, right], a_next)
        start(unit, "a2-L", dst.at[r, a3, :, :, left], rec_r[g].at[r, :, :, left], a_prev)

    def stage1(unit):
        r, g = unit
        left, right = RS_LEFT[g], RS_RIGHT[g]
        ref, from_a, from_b = part[g], rec_a[g], rec_b[g]
        arrived(unit, "a1+", "a1-")

        def put_left(i, n, width, value):
            ref[r, a1, i, :, pl.ds(n, width)] = value

        add(
            4, 0, left.size, put_left,
            lambda i, n, width: ref[r, a1, i, :, pl.ds(n, width)],
            lambda i, n, width: from_a[r, i, :, pl.ds(n, width)],
        )
        start(unit, "a2+L", ref.at[r, a1, :, :, left], rec_l[g].at[r, :, :, left], a_next)

        def put_right(i, n, width, value):
            ref[r, a3, i, :, pl.ds(n, width)] = value

        add(
            4, right.start, right.size, put_right,
            lambda i, n, width: ref[r, a3, i, :, pl.ds(n, width)],
            lambda i, n, width: from_b[r, i, :, pl.ds(n - right.start, width)],
        )
        start(unit, "a2-R", ref.at[r, a3, :, :, right], rec_r[g].at[r, :, :, right], a_prev)

    def stage2(unit):
        r, g = unit
        left, right = RS_LEFT[g], RS_RIGHT[g]
        ref, from_l, from_r, to = part[g], rec_l[g], rec_r[g], summed[g]
        arrived(unit, "a2+R", "a2-L", "a2+L", "a2-R")

        def put(i, n, width, value):
            to[r, i, :, pl.ds(n, width)] = value

        add(
            4, 0, left.size + right.size, put,
            lambda i, n, width: ref[r, a, i, :, pl.ds(n, width)],
            lambda i, n, width: from_l[r, i, :, pl.ds(n, width)],
            lambda i, n, width: from_r[r, i, :, pl.ds(n, width)],
        )
        start(unit, "b1+", to.at[r, b2, :, left], sec_a[g].at[r], b_next)
        start(unit, "b1-", to.at[r, b2, :, right], sec_b[g].at[r], b_prev)
        start(unit, "b2+R", to.at[r, b1, :, right], sec_l[g].at[r, :, right], b_next)
        start(unit, "b2-L", to.at[r, b3, :, left], sec_r[g].at[r, :, left], b_prev)

    def stage3(unit):
        r, g = unit
        left, right = RS_LEFT[g], RS_RIGHT[g]
        ref = summed[g]
        arrived(unit, "b1+", "b1-")
        value = ref[r, b1, :, left].astype(F32) + sec_a[g][r].astype(F32)
        ref[r, b1, :, left] = value.astype(BF)
        start(unit, "b2+L", ref.at[r, b1, :, left], sec_l[g].at[r, :, left], b_next)
        value = ref[r, b3, :, right].astype(F32) + sec_b[g][r].astype(F32)
        ref[r, b3, :, right] = value.astype(BF)
        start(unit, "b2-R", ref.at[r, b3, :, right], sec_r[g].at[r, :, right], b_prev)

    def stage4(unit):
        r, g = unit
        arrived(unit, "b2+R", "b2-L", "b2+L", "b2-R")

        def total(k):
            cols = pl.ds(k * HALF, HALF)
            value = summed[g][r, b, :, cols].astype(F32) + sec_l[g][r, :, cols].astype(F32)
            return (value + sec_r[g][r, :, cols].astype(F32)).astype(BF)

        low, high = pl.ds(0, HALF), pl.ds(HALF, HALF)
        if g == 0:
            gate_bf, up_bf = total(0), total(1)
            acts[r, :, low] = gate_bf
            acts[r, :, high] = up_bf
            gate, up = gate_bf.astype(F32), up_bf.astype(F32)
            own[0][r, a, b] = (gate * jax.nn.sigmoid(gate) * up).astype(BF)
        else:
            gate, up, grad = acts[r, :, low].astype(F32), acts[r, :, high].astype(F32), total(0).astype(F32)
            sig = jax.nn.sigmoid(gate)
            own[1][r, a, b, :, low] = (grad * up * sig * (1.0 + gate * (1.0 - sig))).astype(BF)
            own[1][r, a, b, :, high] = (grad * gate * sig).astype(BF)
        start(unit, "c1+", own[g].at[r, a, b], own[g].at[r, a, b], b_next)
        start(unit, "c1-", own[g].at[r, a, b], own[g].at[r, a, b], b_prev)

    def stage5(unit):
        r, g = unit
        left, right = AG_LEFT[g], AG_RIGHT[g]
        arrived(unit, "c1+", "c1-")
        start(unit, "c2+", own[g].at[r, a, b3, :, left], own[g].at[r, a, b3, :, left], b_next)
        start(unit, "c2-", own[g].at[r, a, b1, :, right], own[g].at[r, a, b1, :, right], b_prev)

    def share(unit, name, k):
        r, g = unit
        start(unit, name, own[g].at[r, k], other[g].at[r, :, k], partner)

    def stage6(unit):
        r, g = unit
        arrived(unit, "c2+", "c2-")
        start(unit, "d1+", own[g].at[r, a], own[g].at[r, a], a_next)
        start(unit, "d1-", own[g].at[r, a], own[g].at[r, a], a_prev)
        share(unit, "s0", a)

    def stage7(unit):
        r, g = unit
        left, right = AG_LEFT[g], AG_RIGHT[g]
        arrived(unit, "d1+", "d1-")
        start(unit, "d2+", own[g].at[r, a3, :, :, left], own[g].at[r, a3, :, :, left], a_next)
        start(unit, "d2-", own[g].at[r, a1, :, :, right], own[g].at[r, a1, :, :, right], a_prev)
        share(unit, "s1", a1)
        share(unit, "s3", a3)

    def stage8(unit):
        arrived(unit, "d2+", "d2-")
        share(unit, "s2", a2)

    def stage9(unit):
        r, g = unit
        arrived(unit, "s0", "s1", "s3", "s2")
        ours, rest = flat(own[g][r]), flat(other[g][r])
        if g == 0:
            use("theirs_down")
            total = dot(ours, dw[core]) + dot(rest, dw[1 - core])
        else:
            use("theirs_gate", "theirs_up")
            total = dot_t(ours, gu[core]) + dot_t(rest, gu[1 - core])
        z_part[g, r] = total.astype(BF).reshape((RING, RING, ROWS, WIDTH))
        if unit not in TREE:
            for j in (4, 3, 5, 2, 6, 1, 7):
                start(unit, f"e{j}", piece(z_part, unit, j), z_rec.at[g, r, j - 1], others[j - 1])
            return
        start(unit, "e3", piece(z_part, unit, 5), z_rec.at[g, r, 2], others[6])
        start(unit, "e5", piece(z_part, unit, 3), z_rec.at[g, r, 3], others[0])
        start(unit, "e4a", piece(z_part, unit, 4).at[0], z_rec.at[g, r, 4, 0], others[5])
        start(unit, "e4b", piece(z_part, unit, 4).at[1], z_rec.at[g, r, 4, 1], others[1])
        start(unit, "e1", piece(z_part, unit, 1), z_rec.at[g, r, 0], others[0])
        start(unit, "e7", piece(z_part, unit, 7), z_rec.at[g, r, 1], others[6])

    def piece(ref, unit, by):
        r, g = unit
        target = (z + by) % N_Z
        return ref.at[g, r, target // 2, pl.ds((target % 2) * 2, 2)]

    def stage15(unit):
        r, g = unit
        arrived(unit, "e3", "e5", "e4a", "e4b")
        for by, slot, half in ((6, 2, 0), (2, 3, 1)):
            here = piece(z_part, unit, by)
            total = here[...].astype(F32) + z_rec[g, r, slot].astype(F32)
            both = [total[0], total[1]]
            both[half] = both[half] + z_rec[g, r, 4, half].astype(F32)
            here[0] = both[0].astype(BF)
            here[1] = both[1].astype(BF)
        start(unit, "e6", piece(z_part, unit, 6), z_rec.at[g, r, 5], others[5])
        start(unit, "e2", piece(z_part, unit, 2), z_rec.at[g, r, 6], others[1])

    def stage10(unit):
        r, g = unit
        tree = unit in TREE
        total = piece(z_part, unit, 0)[...].astype(F32)
        if tree:
            arrived(unit, "e1", "e7", "e2", "e6")
        else:
            arrived(unit, *[f"e{j}" for j in range(1, N_Z)])
        for j in (0, 1, 5, 6) if tree else range(N_Z - 1):
            total = total + z_rec[g, r, j].astype(F32)
        here = piece(z_sum, unit, 0)
        here[...] = total.astype(BF)
        for j in (2, 6, 1, 7) if tree else (4, 3, 5, 2, 6, 1, 7):
            start(unit, f"f{j}", here, here, others[j - 1])

    def stage16(unit):
        arrived(unit, "f2", "f6")
        far = piece(z_sum, unit, 6)
        start(unit, "f3", far, far, others[0])
        start(unit, "f4a", far.at[0], far.at[0], others[1])
        far = piece(z_sum, unit, 2)
        start(unit, "f5", far, far, others[6])
        start(unit, "f4b", far.at[1], far.at[1], others[5])

    def stage11(unit):
        if unit in TREE:
            arrived(unit, "f1", "f7", "f3", "f5", "f4a", "f4b")
        else:
            arrived(unit, *[f"f{j}" for j in range(1, N_Z)])

    def tall(held, cols):
        return held[:, :, :, :, cols].reshape((CHUNKS * BLOCK, cols.size))

    def stage12(unit):
        k = unit[0]
        held = (own, other)[k][0]
        c = cot_t[...]
        for n in range(0, HALF, 256):
            cols = pl.ds(n, min(256, HALF - n))
            grads_d[k, cols, :] = dot(c, tall(held, cols)).T.astype(BF)

    def stage13(unit):
        k = unit[0]
        held = (own, other)[k][1]
        t = tok_t[...]
        for n in range(7):
            cols = pl.ds(n * 256, 256)
            grads[k, :, cols] = dot(t, tall(held, cols)).astype(BF)

    def stage14(unit):
        use("tok0", "tok1", "cot0", "cot1")
        tok_t[...] = tok[...].reshape((CHUNKS * BLOCK, WIDTH)).T
        cot_t[...] = cot[...].reshape((CHUNKS * BLOCK, WIDTH)).T

    stages = [
        stage0, stage1, stage2, stage3, stage4, stage5, stage6, stage7, stage8, stage9, stage10, stage11,
        stage12, stage13, stage14, stage15, stage16,
    ]
    for i, r, g in ORDER:
        stages[i]((r, g))
    for copy in swaps:
        copy.wait_send()
    for copy in flows.values():
        copy.wait_send()
    use(*list(waits))


def write_out(z_sum, grads, grads_d, out, tok_grad, gate_grad, up_grad, down_grad, sems):
    core = lax.axis_index("row") % 2
    copies = []

    def copy(src, dst):
        copies.append(pltpu.make_async_copy(src, dst, sems.at[len(copies)]))

    for k, half in enumerate((core, 1 - core)):
        cols = pl.ds(pl.multiple_of(half * HALF, 128), HALF)
        copy(grads.at[k, :, pl.ds(0, HALF)], gate_grad.at[:, cols])
        copy(grads.at[k, :, pl.ds(HALF, HALF)], up_grad.at[:, cols])
        copy(grads_d.at[k], down_grad.at[half])
    for each in copies:
        each.start()
    for g, array in enumerate((out, tok_grad)):
        copy(z_sum.at[g], array)

        @pl.when(core == 0)
        def _():
            copies[-1].start()

        @pl.when(core == 1)
        def _():
            for k in range(4):
                pltpu.make_async_copy(z_sum.at[g, :, k], array.at[:, :, k], sems.at[len(copies) - 1]).start()

    for each in copies:
        each.wait()


def per_device(tokens, gate_weight, up_weight, down_weight, cotangent):
    rows = (CHUNKS, RING, RING, ROWS, WIDTH)
    grad = (CHUNKS, RING, RING, ROWS)
    V = pltpu.VMEM

    def pair(shape, cols):
        return tuple(V(shape + (n,), BF) for n in cols)

    S = jax.ShapeDtypeStruct
    hbm, vmem = pl.BlockSpec(memory_space=pltpu.HBM), pl.BlockSpec(memory_space=pltpu.VMEM)
    results = pl.pallas_call(
        kernel,
        out_shape=(V((2,) + rows, BF), V((2, WIDTH, 2 * HALF), BF), V((2, HALF, WIDTH), BF)),
        in_specs=[hbm] * 5,
        out_specs=[vmem] * 3,
        scratch_shapes=[
            V(rows, BF), V(rows, BF), V(rows, BF), V(rows, BF),
            V((2, WIDTH, 2 * HALF), BF), V((WIDTH, 2 * HALF), BF),
            V((2, HALF, WIDTH), BF), V((HALF, WIDTH), BF),
            V((WIDTH, CHUNKS * BLOCK), BF), V((WIDTH, CHUNKS * BLOCK), BF),
            pair(grad, (2 * HALF, HALF)),
            pair((CHUNKS, RING, ROWS), (896, 512)),
            pair((CHUNKS, RING, ROWS), (896, 384)),
            pair((CHUNKS, RING, ROWS), (2 * HALF, HALF)), pair((CHUNKS, RING, ROWS), (2 * HALF, HALF)),
            pair((CHUNKS, RING, ROWS), (2 * HALF, HALF)),
            pair((CHUNKS, ROWS), (896, 512)), pair((CHUNKS, ROWS), (896, 384)),
            pair((CHUNKS, ROWS), (2 * HALF, HALF)), pair((CHUNKS, ROWS), (2 * HALF, HALF)),
            V((CHUNKS, ROWS, 2 * HALF), BF),
            pair(grad, (HALF, 2 * HALF)), pair(grad, (HALF, 2 * HALF)),
            V((2,) + rows, BF),
            V((2, CHUNKS, N_Z - 1, 2, ROWS, WIDTH), BF),
            pltpu.SemaphoreType.DMA((2 * CHUNKS, N_SEMS)), pltpu.SemaphoreType.DMA((2 * CHUNKS, N_SEMS)),
            pltpu.SemaphoreType.DMA((8,)), pltpu.SemaphoreType.DMA((8,)),
            pltpu.SemaphoreType.DMA((24,)),
        ],
        compiler_params=pltpu.CompilerParams(
            collective_id=0, has_side_effects=True, vmem_limit_bytes=60 << 20
        ),
    )(
        tokens.reshape(rows), gate_weight, up_weight, down_weight.reshape((2, HALF, WIDTH)), cotangent.reshape(rows),
    )
    output, tokens_grad, gate_grad, up_grad, down_grad = pl.pallas_call(
        write_out,
        out_shape=(
            S(rows, BF), S(rows, BF), S((WIDTH, 2 * HALF), BF), S((WIDTH, 2 * HALF), BF), S((2, HALF, WIDTH), BF),
        ),
        in_specs=[vmem] * 3,
        out_specs=[hbm] * 5,
        scratch_shapes=[pltpu.SemaphoreType.DMA((8,))],
    )(*results)
    return (
        output.reshape(tokens.shape), tokens_grad.reshape(tokens.shape), gate_grad, up_grad,
        down_grad.reshape(down_weight.shape),
    )


def solution(mesh):
    return jax.shard_map(
        per_device,
        mesh=mesh,
        in_specs=(
            P(None, "row"),
            P("row", "col"),
            P("row", "col"),
            P("col", "row"),
            P(None, "row"),
        ),
        out_specs=(
            P(None, "row"),
            P(None, "row"),
            P("row", "col"),
            P("row", "col"),
            P("col", "row"),
        ),
        check_vma=False,
    )
```

```python
import itertools

import jax
import jax.numpy as jnp
from jax import lax
from jax.experimental import pallas as pl
from jax.experimental.pallas import tpu as pltpu
from jax.sharding import PartitionSpec as P

MESH = pl.DeviceIdType.MESH
BF, F32 = jnp.bfloat16, jnp.float32
CHUNKS, RING, ROWS, N_Z = 4, 4, 16, 8
BLOCK = RING * RING * ROWS
WIDTH, HALF = 256, 896
KINDS = ("a1", "a2", "b1", "b2", "c1", "c2", "d1", "d2", "s", "e1", "e2", "f1", "f2")
SENDS = "efabcds"
TREE = {(0, 1), (2, 1), (0, 0), (1, 1), (2, 0), (3, 0), (1, 0)}
Z_PEERS = (1, 2, 3, 4, 5, 6, 7)
RS_LEFT, RS_RIGHT = (pl.ds(0, 896), pl.ds(0, 512)), (pl.ds(896, 896), pl.ds(512, 384))
AG_LEFT, AG_RIGHT = (pl.ds(0, 512), pl.ds(0, 896)), (pl.ds(512, 384), pl.ds(896, 896))

ORDER = [
    (0, 0, 0), (0, 0, 1), (14, 0, 0), (0, 1, 0), (1, 0, 0), (1, 0, 1), (0, 1, 1), (1, 1, 0),
    (0, 2, 0), (2, 0, 0), (2, 0, 1), (1, 1, 1), (2, 1, 0), (0, 2, 1), (1, 2, 0), (3, 0, 0),
    (3, 0, 1), (0, 3, 0), (3, 1, 0), (2, 1, 1), (1, 2, 1), (2, 2, 0), (4, 0, 0), (4, 0, 1),
    (1, 3, 0), (4, 1, 0), (3, 1, 1), (0, 3, 1), (2, 2, 1), (3, 2, 0), (5, 0, 0), (5, 0, 1),
    (2, 3, 0), (5, 1, 0), (4, 1, 1), (1, 3, 1), (3, 2, 1), (4, 2, 0), (6, 0, 0), (6, 0, 1),
    (3, 3, 0), (6, 1, 0), (5, 1, 1), (2, 3, 1), (4, 2, 1), (5, 2, 0), (7, 0, 0), (7, 0, 1),
    (4, 3, 0), (7, 1, 0), (6, 1, 1), (3, 3, 1), (5, 2, 1), (6, 2, 0), (8, 0, 0), (8, 0, 1),
    (9, 0, 0), (5, 3, 0), (8, 1, 0), (9, 0, 1), (9, 1, 0), (7, 1, 1), (4, 3, 1), (15, 0, 0),
    (6, 2, 1), (7, 2, 0), (15, 0, 1), (6, 3, 0), (15, 1, 0), (8, 1, 1), (10, 0, 0), (5, 3, 1),
    (9, 1, 1), (10, 0, 1), (10, 1, 0), (7, 2, 1), (8, 2, 0), (16, 0, 0), (7, 3, 0), (9, 2, 0),
    (6, 3, 1), (15, 1, 1), (16, 0, 1), (8, 2, 1), (16, 1, 0), (8, 3, 0), (9, 2, 1), (11, 0, 0),
    (9, 3, 0), (15, 2, 0), (12, 0, 0), (7, 3, 1), (10, 1, 1), (11, 0, 1), (11, 1, 0), (12, 1, 0),
    (15, 2, 1), (15, 3, 0), (8, 3, 1), (10, 2, 0), (16, 1, 1), (9, 3, 1), (10, 2, 1), (13, 0, 1),
    (10, 3, 0), (16, 2, 0), (11, 1, 1), (13, 1, 1), (10, 3, 1), (16, 2, 1), (16, 3, 0), (11, 2, 0),
    (11, 3, 1), (11, 2, 1), (11, 3, 0),]


def dot(left, right):
    return jnp.dot(left, right, preferred_element_type=F32)


def dot_t(left, right):
    return lax.dot_general(left, right, (((1,), (1,)), ((), ())), preferred_element_type=F32)


def kernel(
    tok_in, gw_in, uw_in, dw_in, cot_in,
    z_sum, grads, grads_d,
    tok, cot, tok_p, cot_p, gu, gu_p, dw, dw_p, tok_t, cot_t,
    part, rec_in, rec_out, summed, sec_in, sec_out,
    acts, own, other, z_part, z_rec,
    send, recv, swap_send, swap_recv, local,
):
    row, z = lax.axis_index("row"), lax.axis_index("col")
    y, x, core = row // 8, (row // 2) % 4, row % 2
    a = x + core * (y - x)
    b = y + core * (x - y)

    def step_a(by):
        return (
            ((y + core * by + 4) % 4) * 8 + ((x + (1 - core) * by + 4) % 4) * 2 + core,
            z,
        )

    def step_b(by):
        return (
            ((y + (1 - core) * by + 4) % 4) * 8 + ((x + core * by + 4) % 4) * 2 + core,
            z,
        )

    a_next, a_prev, b_next, b_prev = step_a(1), step_a(-1), step_b(1), step_b(-1)
    partner = (y * 8 + x * 2 + 1 - core, z)
    others = [(row, (z + j) % N_Z) for j in range(1, N_Z)]
    a1, a2, a3 = (a + 1) % 4, (a + 2) % 4, (a + 3) % 4
    b1, b2, b3 = (b + 1) % 4, (b + 2) % 4, (b + 3) % 4
    theirs = pl.multiple_of((1 - core) * HALF, 128)

    waits, counter = {}, itertools.count()

    def rows_of(ref, first, count):
        return ref.at[pl.ds(first, count)]

    def load(name, src, dst):
        copy = pltpu.make_async_copy(src, dst, local.at[next(counter)])
        waits[name] = copy.wait
        copy.start()

    def load_rows(name, src, dst, first, count):
        sem = local.at[next(counter)]
        waits[name] = pltpu.make_async_copy(rows_of(src, first, count), rows_of(dst, first, count), sem).wait

        @pl.when(core == 0)
        def _():
            pltpu.make_async_copy(rows_of(src, first, count), rows_of(dst, first, count), sem).start()

        @pl.when(core == 1)
        def _():
            for k in range(4):
                pltpu.make_async_copy(
                    src.at[pl.ds(first, count), :, k], dst.at[pl.ds(first, count), k], sem
                ).start()

    def use(*names):
        for name in names:
            if name in waits:
                waits.pop(name)()

    def load_weights(name, half):
        cols = pl.ds(pl.multiple_of(half * HALF, 128), HALF)
        load(name + "_gate", gw_in.at[:, cols], gu.at[half, :, pl.ds(0, HALF)])
        load(name + "_up", uw_in.at[:, cols], gu.at[half, :, pl.ds(HALF, HALF)])
        load(name + "_down", dw_in.at[half], dw.at[half])

    load_rows("tok0", tok_in, tok, 0, 1)
    load_weights("mine", core)
    load_rows("cot0", cot_in, cot, 0, 1)

    barrier = pltpu.get_barrier_semaphore()
    peers = [partner, a_next, a_prev, b_next, b_prev] + [others[j - 1] for j in Z_PEERS]
    for peer in peers:
        pl.semaphore_signal(barrier, inc=1, device_id=peer, device_id_type=MESH)
    pl.semaphore_wait(barrier, len(peers))

    def remote(src, dst, s, r, to):
        return pltpu.make_async_remote_copy(
            src_ref=src, dst_ref=dst, send_sem=s, recv_sem=r, device_id=to, device_id_type=MESH
        )

    swaps = []

    def swap(name, src, dst):
        copy = remote(src, dst, swap_send.at[len(swaps)], swap_recv.at[len(swaps)], partner)
        swaps.append(copy)
        waits[name] = copy.wait_recv
        copy.start()

    def swap_rows(name, src, dst, first, count):
        i = len(swaps)

        def part_copy(src, dst):
            return remote(src, dst, swap_send.at[i], swap_recv.at[i], partner)

        whole = part_copy(rows_of(src, first, count), rows_of(dst, first, count))
        swaps.append(whole)
        waits[name] = whole.wait_recv

        @pl.when(core == 1)
        def _():
            whole.start()

        @pl.when(core == 0)
        def _():
            for k in range(4):
                part_copy(src.at[pl.ds(first, count), :, k], dst.at[pl.ds(first, count), k]).start()

    swap_rows("tok_p0", tok_in, tok_p, 0, 1)
    swap("gate_p", gw_in.at[:, pl.ds(theirs, HALF)], gu_p.at[:, pl.ds(0, HALF)])
    swap("up_p", uw_in.at[:, pl.ds(theirs, HALF)], gu_p.at[:, pl.ds(HALF, HALF)])
    swap_rows("cot_p0", cot_in, cot_p, 0, 1)
    swap("down_p", dw_in.at[1 - core], dw_p)
    swap_rows("tok_p1", tok_in, tok_p, 1, CHUNKS - 1)
    swap_rows("cot_p1", cot_in, cot_p, 1, CHUNKS - 1)
    load_rows("tok1", tok_in, tok, 1, CHUNKS - 1)
    load_rows("cot1", cot_in, cot, 1, CHUNKS - 1)
    load_weights("theirs", 1 - core)

    def start(unit, kind, src, dst, to):
        r, g = unit
        place = SENDS.index(kind[0])
        out_sem = place if place < 2 else 2 * place - 2 + g
        remote(src, dst, send.at[out_sem], recv.at[KINDS.index(kind), 2 * r + g], to).start()

    def arrived(unit, kind, ref):
        r, g = unit
        remote(ref, ref, send.at[0], recv.at[KINDS.index(kind), 2 * r + g], partner).wait_recv()

    def flat(value):
        return value.reshape((BLOCK, value.shape[-1]))

    def add(blocks, begin, size, into, *terms):
        width = min(size, HALF)

        def step(i, carry):
            for n in range(begin, begin + size, width):
                total = terms[0](i, n, width).astype(F32)
                for term in terms[1:]:
                    total = total + term(i, n, width).astype(F32)
                into(i, n, width, total.astype(BF))
            return carry

        lax.fori_loop(0, blocks, step, 0)

    def stage0(unit):
        r, g = unit
        late = "" if r == 0 else "1"
        if g == 0:
            use("tok0", "mine_gate", "mine_up", "tok_p0", "gate_p", "up_p", "tok" + late, "tok_p" + late)
        else:
            use("cot0", "mine_down", "cot_p0", "down_p", "cot" + late, "cot_p" + late)
        dst = part[g]
        if g == 0:
            t, tp = flat(tok[r]), flat(tok_p[r])
            for n in range(0, 2 * HALF, 256):
                cols = pl.ds(n, 256)
                total = dot(t, gu[core, :, cols]) + dot(tp, gu_p[:, cols])
                dst[r, :, :, :, cols] = total.astype(BF).reshape((RING, RING, ROWS, 256))
        else:
            c, cp = flat(cot[r]), flat(cot_p[r])
            for n in range(0, HALF, 256):
                size = min(256, HALF - n)
                units = pl.ds(n, size)
                total = dot_t(c, dw[core, units, :]) + dot_t(cp, dw_p[units, :])
                dst[r, :, :, :, units] = total.astype(BF).reshape((RING, RING, ROWS, size))
        left, right = RS_LEFT[g], RS_RIGHT[g]
        start(unit, "a1", dst.at[r, a2, :, :, left], rec_in[g].at[r, :, :, left], a_next)
        start(unit, "a1", dst.at[r, a2, :, :, right], rec_in[g].at[r, :, :, right], a_prev)
        start(unit, "a2", dst.at[r, a1, :, :, right], rec_out[g].at[r, 0, :, :, right], a_next)
        start(unit, "a2", dst.at[r, a3, :, :, left], rec_out[g].at[r, 1, :, :, left], a_prev)

    def stage1(unit):
        r, g = unit
        left, right = RS_LEFT[g], RS_RIGHT[g]
        ref, held = part[g], rec_in[g]
        arrived(unit, "a1", held.at[r])

        def put_left(i, n, width, value):
            ref[r, a1, i, :, pl.ds(n, width)] = value

        add(
            4, 0, left.size, put_left,
            lambda i, n, width: ref[r, a1, i, :, pl.ds(n, width)],
            lambda i, n, width: held[r, i, :, pl.ds(n, width)],
        )
        start(unit, "a2", ref.at[r, a1, :, :, left], rec_out[g].at[r, 0, :, :, left], a_next)

        def put_right(i, n, width, value):
            ref[r, a3, i, :, pl.ds(n, width)] = value

        add(
            4, right.start, right.size, put_right,
            lambda i, n, width: ref[r, a3, i, :, pl.ds(n, width)],
            lambda i, n, width: held[r, i, :, pl.ds(n, width)],
        )
        start(unit, "a2", ref.at[r, a3, :, :, right], rec_out[g].at[r, 1, :, :, right], a_prev)

    def stage2(unit):
        r, g = unit
        left, right = RS_LEFT[g], RS_RIGHT[g]
        ref, held, to = part[g], rec_out[g], summed[g]
        arrived(unit, "a2", held.at[r])

        def put(i, n, width, value):
            to[r, i, :, pl.ds(n, width)] = value

        add(
            4, 0, left.size + right.size, put,
            lambda i, n, width: ref[r, a, i, :, pl.ds(n, width)],
            lambda i, n, width: held[r, 0, i, :, pl.ds(n, width)],
            lambda i, n, width: held[r, 1, i, :, pl.ds(n, width)],
        )
        start(unit, "b1", to.at[r, b2, :, left], sec_in[g].at[r, :, left], b_next)
        start(unit, "b1", to.at[r, b2, :, right], sec_in[g].at[r, :, right], b_prev)
        start(unit, "b2", to.at[r, b1, :, right], sec_out[g].at[r, 0, :, right], b_next)
        start(unit, "b2", to.at[r, b3, :, left], sec_out[g].at[r, 1, :, left], b_prev)

    def stage3(unit):
        r, g = unit
        left, right = RS_LEFT[g], RS_RIGHT[g]
        ref = summed[g]
        arrived(unit, "b1", sec_in[g].at[r])
        value = ref[r, b1, :, left].astype(F32) + sec_in[g][r, :, left].astype(F32)
        ref[r, b1, :, left] = value.astype(BF)
        start(unit, "b2", ref.at[r, b1, :, left], sec_out[g].at[r, 0, :, left], b_next)
        value = ref[r, b3, :, right].astype(F32) + sec_in[g][r, :, right].astype(F32)
        ref[r, b3, :, right] = value.astype(BF)
        start(unit, "b2", ref.at[r, b3, :, right], sec_out[g].at[r, 1, :, right], b_prev)

    def stage4(unit):
        r, g = unit
        arrived(unit, "b2", sec_out[g].at[r])

        def total(k):
            cols = pl.ds(k * HALF, HALF)
            value = summed[g][r, b, :, cols].astype(F32) + sec_out[g][r, 0, :, cols].astype(F32)
            return (value + sec_out[g][r, 1, :, cols].astype(F32)).astype(BF)

        low, high = pl.ds(0, HALF), pl.ds(HALF, HALF)
        if g == 0:
            gate_bf, up_bf = total(0), total(1)
            acts[r, :, low] = gate_bf
            acts[r, :, high] = up_bf
            gate, up = gate_bf.astype(F32), up_bf.astype(F32)
            own[0][r, a, b] = (gate * jax.nn.sigmoid(gate) * up).astype(BF)
        else:
            gate, up, grad = acts[r, :, low].astype(F32), acts[r, :, high].astype(F32), total(0).astype(F32)
            sig = jax.nn.sigmoid(gate)
            own[1][r, a, b, :, low] = (grad * up * sig * (1.0 + gate * (1.0 - sig))).astype(BF)
            own[1][r, a, b, :, high] = (grad * gate * sig).astype(BF)
        start(unit, "c1", own[g].at[r, a, b], own[g].at[r, a, b], b_next)
        start(unit, "c1", own[g].at[r, a, b], own[g].at[r, a, b], b_prev)

    def stage5(unit):
        r, g = unit
        left, right = AG_LEFT[g], AG_RIGHT[g]
        arrived(unit, "c1", own[g].at[r, a, pl.ds(0, 2)])
        start(unit, "c2", own[g].at[r, a, b3, :, left], own[g].at[r, a, b3, :, left], b_next)
        start(unit, "c2", own[g].at[r, a, b1, :, right], own[g].at[r, a, b1, :, right], b_prev)

    def share(unit, k):
        r, g = unit
        start(unit, "s", own[g].at[r, k], other[g].at[r, :, k], partner)

    def stage6(unit):
        r, g = unit
        arrived(unit, "c2", own[g].at[r, a, b2])
        start(unit, "d1", own[g].at[r, a], own[g].at[r, a], a_next)
        start(unit, "d1", own[g].at[r, a], own[g].at[r, a], a_prev)
        share(unit, a)

    def stage7(unit):
        r, g = unit
        left, right = AG_LEFT[g], AG_RIGHT[g]
        arrived(unit, "d1", own[g].at[r, pl.ds(0, 2)])
        start(unit, "d2", own[g].at[r, a3, :, :, left], own[g].at[r, a3, :, :, left], a_next)
        start(unit, "d2", own[g].at[r, a1, :, :, right], own[g].at[r, a1, :, :, right], a_prev)
        share(unit, a1)
        share(unit, a3)

    def stage8(unit):
        r, g = unit
        arrived(unit, "d2", own[g].at[r, a2])
        share(unit, a2)

    def stage9(unit):
        r, g = unit
        arrived(unit, "s", other[g].at[r])
        ours, rest = flat(own[g][r]), flat(other[g][r])
        if g == 0:
            use("theirs_down")
            total = dot(ours, dw[core]) + dot(rest, dw[1 - core])
        else:
            use("theirs_gate", "theirs_up")
            total = dot_t(ours, gu[core]) + dot_t(rest, gu[1 - core])
        z_part[g, r] = total.astype(BF).reshape((RING, RING, ROWS, WIDTH))
        if unit not in TREE:
            for j in (4, 3, 5, 2, 6, 1, 7):
                start(unit, "e1", piece(z_part, unit, j), z_rec.at[g, r, j - 1], others[j - 1])
            return
        start(unit, "e1", piece(z_part, unit, 5), z_rec.at[g, r, 0], others[6])
        start(unit, "e1", piece(z_part, unit, 3), z_rec.at[g, r, 1], others[0])
        start(unit, "e1", piece(z_part, unit, 4).at[0], z_rec.at[g, r, 2, 0], others[5])
        start(unit, "e1", piece(z_part, unit, 4).at[1], z_rec.at[g, r, 2, 1], others[1])
        start(unit, "e2", piece(z_part, unit, 1), z_rec.at[g, r, 3], others[0])
        start(unit, "e2", piece(z_part, unit, 7), z_rec.at[g, r, 4], others[6])

    def piece(ref, unit, by):
        r, g = unit
        target = (z + by) % N_Z
        return ref.at[g, r, target // 2, pl.ds((target % 2) * 2, 2)]

    def stage15(unit):
        r, g = unit
        arrived(unit, "e1", z_rec.at[g, r, pl.ds(0, 3)])
        for by, slot, half in ((6, 0, 0), (2, 1, 1)):
            here = piece(z_part, unit, by)
            total = here[...].astype(F32) + z_rec[g, r, slot].astype(F32)
            both = [total[0], total[1]]
            both[half] = both[half] + z_rec[g, r, 2, half].astype(F32)
            here[0] = both[0].astype(BF)
            here[1] = both[1].astype(BF)
        start(unit, "e2", piece(z_part, unit, 6), z_rec.at[g, r, 5], others[5])
        start(unit, "e2", piece(z_part, unit, 2), z_rec.at[g, r, 6], others[1])

    def stage10(unit):
        r, g = unit
        tree = unit in TREE
        total = piece(z_part, unit, 0)[...].astype(F32)
        if tree:
            arrived(unit, "e2", z_rec.at[g, r, pl.ds(3, 4)])
        else:
            arrived(unit, "e1", z_rec.at[g, r])
        for j in (3, 4, 5, 6) if tree else range(N_Z - 1):
            total = total + z_rec[g, r, j].astype(F32)
        here = piece(z_sum, unit, 0)
        here[...] = total.astype(BF)
        for j in (2, 6, 1, 7) if tree else (4, 3, 5, 2, 6, 1, 7):
            start(unit, "f1" if j in (2, 6) or not tree else "f2", here, here, others[j - 1])

    def stage16(unit):
        r, g = unit
        arrived(unit, "f1", z_rec.at[g, r, pl.ds(0, 2)])
        far = piece(z_sum, unit, 6)
        start(unit, "f2", far, far, others[0])
        start(unit, "f2", far.at[0], far.at[0], others[1])
        far = piece(z_sum, unit, 2)
        start(unit, "f2", far, far, others[6])
        start(unit, "f2", far.at[1], far.at[1], others[5])

    def stage11(unit):
        r, g = unit
        if unit in TREE:
            arrived(unit, "f2", z_rec.at[g, r, pl.ds(0, 5)])
        else:
            arrived(unit, "f1", z_rec.at[g, r])

    def tall(held, cols):
        return held[:, :, :, :, cols].reshape((CHUNKS * BLOCK, cols.size))

    def stage12(unit):
        k = unit[0]
        held = (own, other)[k][0]
        c = cot_t[...]
        for n in range(0, HALF, 256):
            cols = pl.ds(n, min(256, HALF - n))
            grads_d[k, cols, :] = dot(c, tall(held, cols)).T.astype(BF)

    def stage13(unit):
        k = unit[0]
        held = (own, other)[k][1]
        t = tok_t[...]
        for n in range(7):
            cols = pl.ds(n * 256, 256)
            grads[k, :, cols] = dot(t, tall(held, cols)).astype(BF)

    def stage14(unit):
        use("tok0", "tok1", "cot0", "cot1")
        tok_t[...] = tok[...].reshape((CHUNKS * BLOCK, WIDTH)).T
        cot_t[...] = cot[...].reshape((CHUNKS * BLOCK, WIDTH)).T

    stages = [
        stage0, stage1, stage2, stage3, stage4, stage5, stage6, stage7, stage8, stage9, stage10, stage11,
        stage12, stage13, stage14, stage15, stage16,
    ]
    for i, r, g in ORDER:
        stages[i]((r, g))
    for copy in swaps:
        copy.wait_send()

    def all_sent(i, ref):
        remote(ref, ref, send.at[i], recv.at[0, 0], partner).wait_send()

    for g in range(2):
        all_sent(g, z_rec)
        all_sent(2 + g, part[g].at[:, pl.ds(0, 3)])
        all_sent(4 + g, part[g].at[:, 0, pl.ds(0, 3)])
        all_sent(6 + g, own[g].at[:, 0, pl.ds(0, 3)])
        all_sent(8 + g, own[g].at[:, pl.ds(0, 3)])
        all_sent(10 + g, own[g])
    use(*list(waits))


def write_out(z_sum, grads, grads_d, out, tok_grad, gate_grad, up_grad, down_grad, sems):
    core = lax.axis_index("row") % 2
    copies = []

    def copy(src, dst):
        copies.append(pltpu.make_async_copy(src, dst, sems.at[len(copies)]))

    for k, half in enumerate((core, 1 - core)):
        cols = pl.ds(pl.multiple_of(half * HALF, 128), HALF)
        copy(grads.at[k, :, pl.ds(0, HALF)], gate_grad.at[:, cols])
        copy(grads.at[k, :, pl.ds(HALF, HALF)], up_grad.at[:, cols])
        copy(grads_d.at[k], down_grad.at[half])
    for each in copies:
        each.start()
    for g, array in enumerate((out, tok_grad)):
        copy(z_sum.at[g], array)

        @pl.when(core == 0)
        def _():
            copies[-1].start()

        @pl.when(core == 1)
        def _():
            for k in range(4):
                pltpu.make_async_copy(z_sum.at[g, :, k], array.at[:, :, k], sems.at[len(copies) - 1]).start()

    for each in copies:
        each.wait()


def per_device(tokens, gate_weight, up_weight, down_weight, cotangent):
    rows = (CHUNKS, RING, RING, ROWS, WIDTH)
    grad = (CHUNKS, RING, RING, ROWS)
    V = pltpu.VMEM

    def pair(shape, cols):
        return tuple(V(shape + (n,), BF) for n in cols)

    S = jax.ShapeDtypeStruct
    hbm, vmem = pl.BlockSpec(memory_space=pltpu.HBM), pl.BlockSpec(memory_space=pltpu.VMEM)
    results = pl.pallas_call(
        kernel,
        out_shape=(V((2,) + rows, BF), V((2, WIDTH, 2 * HALF), BF), V((2, HALF, WIDTH), BF)),
        in_specs=[hbm] * 5,
        out_specs=[vmem] * 3,
        scratch_shapes=[
            V(rows, BF), V(rows, BF), V(rows, BF), V(rows, BF),
            V((2, WIDTH, 2 * HALF), BF), V((WIDTH, 2 * HALF), BF),
            V((2, HALF, WIDTH), BF), V((HALF, WIDTH), BF),
            V((WIDTH, CHUNKS * BLOCK), BF), V((WIDTH, CHUNKS * BLOCK), BF),
            pair(grad, (2 * HALF, HALF)),
            pair((CHUNKS, RING, ROWS), (2 * HALF, HALF)),
            pair((CHUNKS, 2, RING, ROWS), (2 * HALF, HALF)),
            pair((CHUNKS, RING, ROWS), (2 * HALF, HALF)),
            pair((CHUNKS, ROWS), (2 * HALF, HALF)),
            pair((CHUNKS, 2, ROWS), (2 * HALF, HALF)),
            V((CHUNKS, ROWS, 2 * HALF), BF),
            pair(grad, (HALF, 2 * HALF)), pair(grad, (HALF, 2 * HALF)),
            V((2,) + rows, BF),
            V((2, CHUNKS, N_Z - 1, 2, ROWS, WIDTH), BF),
            pltpu.SemaphoreType.DMA((12,)), pltpu.SemaphoreType.DMA((len(KINDS), 2 * CHUNKS)),
            pltpu.SemaphoreType.DMA((7,)), pltpu.SemaphoreType.DMA((7,)), pltpu.SemaphoreType.DMA((10,)),
        ],
        compiler_params=pltpu.CompilerParams(
            collective_id=0, has_side_effects=True, vmem_limit_bytes=60 << 20
        ),
    )(
        tokens.reshape(rows), gate_weight, up_weight, down_weight.reshape((2, HALF, WIDTH)), cotangent.reshape(rows),
    )
    output, tokens_grad, gate_grad, up_grad, down_grad = pl.pallas_call(
        write_out,
        out_shape=(
            S(rows, BF), S(rows, BF), S((WIDTH, 2 * HALF), BF), S((WIDTH, 2 * HALF), BF), S((2, HALF, WIDTH), BF),
        ),
        in_specs=[vmem] * 3,
        out_specs=[hbm] * 5,
        scratch_shapes=[pltpu.SemaphoreType.DMA((8,))],
    )(*results)
    return (
        output.reshape(tokens.shape), tokens_grad.reshape(tokens.shape), gate_grad, up_grad,
        down_grad.reshape(down_weight.shape),
    )


def solution(mesh):
    return jax.shard_map(
        per_device,
        mesh=mesh,
        in_specs=(
            P(None, "row"),
            P("row", "col"),
            P("row", "col"),
            P("col", "row"),
            P(None, "row"),
        ),
        out_specs=(
            P(None, "row"),
            P(None, "row"),
            P("row", "col"),
            P("row", "col"),
            P("col", "row"),
        ),
        check_vma=False,
    )
```

```python
import itertools

import jax
import jax.numpy as jnp
from jax import lax
from jax.experimental import pallas as pl
from jax.experimental.pallas import tpu as pltpu
from jax.sharding import PartitionSpec as P

MESH = pl.DeviceIdType.MESH
BF, F32 = jnp.bfloat16, jnp.float32
CHUNKS, RING, ROWS, N_Z = 4, 4, 16, 8
BLOCK = RING * RING * ROWS
WIDTH, HALF = 256, 896
FAR_B, FAR_C, FAR_A = (), (), ()
KINDS = ("a1", "a2", "b1", "b2", "c1", "c2", "d1", "d2", "s", "e1", "e2", "f1", "f2")
SENDS = "efabcds"
TREE = ((0, 0), (0, 1), (1, 0), (1, 1), (2, 0), (2, 1), (3, 0))
Z_PEERS = (1, 2, 3, 4, 5, 6, 7)
RS_LEFT, RS_RIGHT = (pl.ds(0, 896), pl.ds(0, 512)), (pl.ds(896, 896), pl.ds(512, 384))
AG_LEFT, AG_RIGHT = (pl.ds(0, 512), pl.ds(0, 896)), (pl.ds(512, 384), pl.ds(896, 896))

ORDER = [
    (0, 0, 0), (0, 0, 1), (14, 0, 0), (0, 1, 0), (1, 0, 0), (1, 0, 1), (0, 1, 1), (1, 1, 0),
    (0, 2, 0), (2, 0, 0), (2, 0, 1), (1, 1, 1), (2, 1, 0), (0, 2, 1), (1, 2, 0), (3, 0, 0),
    (3, 0, 1), (0, 3, 0), (3, 1, 0), (2, 1, 1), (1, 2, 1), (2, 2, 0), (4, 0, 0), (4, 0, 1),
    (1, 3, 0), (4, 1, 0), (3, 1, 1), (0, 3, 1), (2, 2, 1), (3, 2, 0), (5, 0, 0), (5, 0, 1),
    (2, 3, 0), (5, 1, 0), (4, 1, 1), (1, 3, 1), (3, 2, 1), (4, 2, 0), (6, 0, 0), (6, 0, 1),
    (3, 3, 0), (6, 1, 0), (5, 1, 1), (2, 3, 1), (4, 2, 1), (5, 2, 0), (7, 0, 0), (7, 0, 1),
    (4, 3, 0), (7, 1, 0), (6, 1, 1), (3, 3, 1), (5, 2, 1), (6, 2, 0), (8, 0, 0), (8, 0, 1),
    (9, 0, 0), (5, 3, 0), (8, 1, 0), (9, 0, 1), (9, 1, 0), (7, 1, 1), (4, 3, 1), (15, 0, 0),
    (6, 2, 1), (7, 2, 0), (15, 0, 1), (6, 3, 0), (15, 1, 0), (8, 1, 1), (10, 0, 0), (5, 3, 1),
    (9, 1, 1), (10, 0, 1), (10, 1, 0), (7, 2, 1), (8, 2, 0), (16, 0, 0), (7, 3, 0), (9, 2, 0),
    (6, 3, 1), (15, 1, 1), (16, 0, 1), (8, 2, 1), (16, 1, 0), (8, 3, 0), (9, 2, 1), (11, 0, 0),
    (9, 3, 0), (15, 2, 0), (12, 0, 0), (7, 3, 1), (10, 1, 1), (11, 0, 1), (11, 1, 0), (12, 1, 0),
    (15, 2, 1), (15, 3, 0), (8, 3, 1), (10, 2, 0), (16, 1, 1), (9, 3, 1), (10, 2, 1), (13, 0, 1),
    (10, 3, 0), (16, 2, 0), (11, 1, 1), (13, 1, 1), (10, 3, 1), (16, 2, 1), (16, 3, 0), (11, 2, 0),
    (11, 3, 1), (11, 2, 1), (11, 3, 0),]


def dot(left, right):
    return jnp.dot(left, right, preferred_element_type=F32)


def dot_t(left, right):
    return lax.dot_general(left, right, (((1,), (1,)), ((), ())), preferred_element_type=F32)


def kernel(
    tok_in, gw_in, uw_in, dw_in, cot_in,
    z_sum, grads, grads_d,
    tok, cot, tok_p, cot_p, gu, gu_p, dw, dw_p, tok_t, cot_t,
    part, rec_in, rec_out, summed, sec_in, sec_out,
    acts, own, other, z_part, z_rec,
    send, recv, swap_send, swap_recv, local,
):
    row, z = lax.axis_index("row"), lax.axis_index("col")
    y, x, core = row // 8, (row // 2) % 4, row % 2
    a = x + core * (y - x)
    b = y + core * (x - y)

    def step_a(by):
        return (
            ((y + core * by + 4) % 4) * 8 + ((x + (1 - core) * by + 4) % 4) * 2 + core,
            z,
        )

    def step_b(by):
        return (
            ((y + (1 - core) * by + 4) % 4) * 8 + ((x + core * by + 4) % 4) * 2 + core,
            z,
        )

    a_next, a_prev, b_next, b_prev = step_a(1), step_a(-1), step_b(1), step_b(-1)
    a_far, b_far = step_a(2), step_b(2)
    partner = (y * 8 + x * 2 + 1 - core, z)
    others = [(row, (z + j) % N_Z) for j in range(1, N_Z)]
    a1, a2, a3 = (a + 1) % 4, (a + 2) % 4, (a + 3) % 4
    b1, b2, b3 = (b + 1) % 4, (b + 2) % 4, (b + 3) % 4
    theirs = pl.multiple_of((1 - core) * HALF, 128)

    waits, counter = {}, itertools.count()

    def rows_of(ref, first, count):
        return ref.at[pl.ds(first, count)]

    def load(name, src, dst):
        copy = pltpu.make_async_copy(src, dst, local.at[next(counter)])
        waits[name] = copy.wait
        copy.start()

    def load_rows(name, src, dst, first, count):
        sem = local.at[next(counter)]
        waits[name] = pltpu.make_async_copy(rows_of(src, first, count), rows_of(dst, first, count), sem).wait

        @pl.when(core == 0)
        def _():
            pltpu.make_async_copy(rows_of(src, first, count), rows_of(dst, first, count), sem).start()

        @pl.when(core == 1)
        def _():
            for k in range(4):
                pltpu.make_async_copy(
                    src.at[pl.ds(first, count), :, k], dst.at[pl.ds(first, count), k], sem
                ).start()

    def use(*names):
        for name in names:
            if name in waits:
                waits.pop(name)()

    def load_weights(name, half):
        cols = pl.ds(pl.multiple_of(half * HALF, 128), HALF)
        load(name + "_gate", gw_in.at[:, cols], gu.at[half, :, pl.ds(0, HALF)])
        load(name + "_up", uw_in.at[:, cols], gu.at[half, :, pl.ds(HALF, HALF)])
        load(name + "_down", dw_in.at[half], dw.at[half])

    load_rows("tok0", tok_in, tok, 0, 1)
    load_weights("mine", core)
    load_rows("cot0", cot_in, cot, 0, 1)

    barrier = pltpu.get_barrier_semaphore()
    peers = [partner, a_next, a_prev, b_next, b_prev] + [a_far] * bool(FAR_A) + [b_far] * bool(FAR_B + FAR_C)
    peers += [others[j - 1] for j in Z_PEERS]
    for peer in peers:
        pl.semaphore_signal(barrier, inc=1, device_id=peer, device_id_type=MESH)
    pl.semaphore_wait(barrier, len(peers))

    def remote(src, dst, s, r, to):
        return pltpu.make_async_remote_copy(
            src_ref=src, dst_ref=dst, send_sem=s, recv_sem=r, device_id=to, device_id_type=MESH
        )

    swaps = []

    def swap(name, src, dst):
        copy = remote(src, dst, swap_send.at[len(swaps)], swap_recv.at[len(swaps)], partner)
        swaps.append(copy)
        waits[name] = copy.wait_recv
        copy.start()

    def swap_rows(name, src, dst, first, count):
        i = len(swaps)

        def part_copy(src, dst):
            return remote(src, dst, swap_send.at[i], swap_recv.at[i], partner)

        whole = part_copy(rows_of(src, first, count), rows_of(dst, first, count))
        swaps.append(whole)
        waits[name] = whole.wait_recv

        @pl.when(core == 1)
        def _():
            whole.start()

        @pl.when(core == 0)
        def _():
            for k in range(4):
                part_copy(src.at[pl.ds(first, count), :, k], dst.at[pl.ds(first, count), k]).start()

    swap_rows("tok_p0", tok_in, tok_p, 0, 1)
    swap("gate_p", gw_in.at[:, pl.ds(theirs, HALF)], gu_p.at[:, pl.ds(0, HALF)])
    swap("up_p", uw_in.at[:, pl.ds(theirs, HALF)], gu_p.at[:, pl.ds(HALF, HALF)])
    swap_rows("cot_p0", cot_in, cot_p, 0, 1)
    swap("down_p", dw_in.at[1 - core], dw_p)
    swap_rows("tok_p1", tok_in, tok_p, 1, CHUNKS - 1)
    swap_rows("cot_p1", cot_in, cot_p, 1, CHUNKS - 1)
    load_rows("tok1", tok_in, tok, 1, CHUNKS - 1)
    load_rows("cot1", cot_in, cot, 1, CHUNKS - 1)
    load_weights("theirs", 1 - core)

    def start(unit, kind, src, dst, to):
        r, g = unit
        place = SENDS.index(kind[0])
        out_sem = place if place < 2 else 2 * place - 2 + g
        remote(src, dst, send.at[out_sem], recv.at[KINDS.index(kind), 2 * r + g], to).start()

    def arrived(unit, kind, ref):
        r, g = unit
        remote(ref, ref, send.at[0], recv.at[KINDS.index(kind), 2 * r + g], partner).wait_recv()

    def flat(value):
        return value.reshape((BLOCK, value.shape[-1]))

    def add(blocks, begin, size, into, *terms):
        width = min(size, HALF)

        def step(i, carry):
            for n in range(begin, begin + size, width):
                total = terms[0](i, n, width).astype(F32)
                for term in terms[1:]:
                    total = total + term(i, n, width).astype(F32)
                into(i, n, width, total.astype(BF))
            return carry

        lax.fori_loop(0, blocks, step, 0)

    def stage0(unit):
        r, g = unit
        late = "" if r == 0 else "1"
        if g == 0:
            use("tok0", "mine_gate", "mine_up", "tok_p0", "gate_p", "up_p", "tok" + late, "tok_p" + late)
        else:
            use("cot0", "mine_down", "cot_p0", "down_p", "cot" + late, "cot_p" + late)
        dst = part[g]
        if g == 0:
            t, tp = flat(tok[r]), flat(tok_p[r])
            for n in range(0, 2 * HALF, 256):
                cols = pl.ds(n, 256)
                total = dot(t, gu[core, :, cols]) + dot(tp, gu_p[:, cols])
                dst[r, :, :, :, cols] = total.astype(BF).reshape((RING, RING, ROWS, 256))
        else:
            c, cp = flat(cot[r]), flat(cot_p[r])
            for n in range(0, HALF, 256):
                size = min(256, HALF - n)
                units = pl.ds(n, size)
                total = dot_t(c, dw[core, units, :]) + dot_t(cp, dw_p[units, :])
                dst[r, :, :, :, units] = total.astype(BF).reshape((RING, RING, ROWS, size))
        left, right = RS_LEFT[g], RS_RIGHT[g]
        start(unit, "a1", dst.at[r, a2, :, :, left], rec_in[g].at[r, :, :, left], a_next)
        start(unit, "a1", dst.at[r, a2, :, :, right], rec_in[g].at[r, :, :, right], a_prev)
        start(unit, "a2", dst.at[r, a1, :, :, right], rec_out[g].at[r, 0, :, :, right], a_next)
        start(unit, "a2", dst.at[r, a3, :, :, left], rec_out[g].at[r, 1, :, :, left], a_prev)

    def stage1(unit):
        r, g = unit
        left, right = RS_LEFT[g], RS_RIGHT[g]
        ref, held = part[g], rec_in[g]
        arrived(unit, "a1", held.at[r])

        def put_left(i, n, width, value):
            ref[r, a1, i, :, pl.ds(n, width)] = value

        add(
            4, 0, left.size, put_left,
            lambda i, n, width: ref[r, a1, i, :, pl.ds(n, width)],
            lambda i, n, width: held[r, i, :, pl.ds(n, width)],
        )
        start(unit, "a2", ref.at[r, a1, :, :, left], rec_out[g].at[r, 0, :, :, left], a_next)

        def put_right(i, n, width, value):
            ref[r, a3, i, :, pl.ds(n, width)] = value

        add(
            4, right.start, right.size, put_right,
            lambda i, n, width: ref[r, a3, i, :, pl.ds(n, width)],
            lambda i, n, width: held[r, i, :, pl.ds(n, width)],
        )
        start(unit, "a2", ref.at[r, a3, :, :, right], rec_out[g].at[r, 1, :, :, right], a_prev)

    def stage2(unit):
        r, g = unit
        left, right = RS_LEFT[g], RS_RIGHT[g]
        ref, held, to = part[g], rec_out[g], summed[g]
        arrived(unit, "a2", held.at[r])

        def put(i, n, width, value):
            to[r, i, :, pl.ds(n, width)] = value

        add(
            4, 0, left.size + right.size, put,
            lambda i, n, width: ref[r, a, i, :, pl.ds(n, width)],
            lambda i, n, width: held[r, 0, i, :, pl.ds(n, width)],
            lambda i, n, width: held[r, 1, i, :, pl.ds(n, width)],
        )
        if unit in FAR_B:
            start(unit, "b1", to.at[r, b2], sec_in[g].at[r], b_far)
            start(unit, "b2", to.at[r, b1], sec_out[g].at[r, 0], b_next)
            start(unit, "b2", to.at[r, b3], sec_out[g].at[r, 1], b_prev)
            return
        start(unit, "b1", to.at[r, b2, :, left], sec_in[g].at[r, :, left], b_next)
        start(unit, "b1", to.at[r, b2, :, right], sec_in[g].at[r, :, right], b_prev)
        start(unit, "b2", to.at[r, b1, :, right], sec_out[g].at[r, 0, :, right], b_next)
        start(unit, "b2", to.at[r, b3, :, left], sec_out[g].at[r, 1, :, left], b_prev)

    def stage3(unit):
        r, g = unit
        left, right = RS_LEFT[g], RS_RIGHT[g]
        ref = summed[g]
        arrived(unit, "b1", sec_in[g].at[r])
        value = ref[r, b1, :, left].astype(F32) + sec_in[g][r, :, left].astype(F32)
        ref[r, b1, :, left] = value.astype(BF)
        start(unit, "b2", ref.at[r, b1, :, left], sec_out[g].at[r, 0, :, left], b_next)
        value = ref[r, b3, :, right].astype(F32) + sec_in[g][r, :, right].astype(F32)
        ref[r, b3, :, right] = value.astype(BF)
        start(unit, "b2", ref.at[r, b3, :, right], sec_out[g].at[r, 1, :, right], b_prev)

    def stage4(unit):
        r, g = unit
        if unit in FAR_B:
            arrived(unit, "b1", sec_in[g].at[r])
        arrived(unit, "b2", sec_out[g].at[r])

        def total(k):
            cols = pl.ds(k * HALF, HALF)
            value = summed[g][r, b, :, cols].astype(F32) + sec_out[g][r, 0, :, cols].astype(F32)
            value = value + sec_out[g][r, 1, :, cols].astype(F32)
            if unit in FAR_B:
                value = value + sec_in[g][r, :, cols].astype(F32)
            return value.astype(BF)

        low, high = pl.ds(0, HALF), pl.ds(HALF, HALF)
        if g == 0:
            gate_bf, up_bf = total(0), total(1)
            acts[r, :, low] = gate_bf
            acts[r, :, high] = up_bf
            gate, up = gate_bf.astype(F32), up_bf.astype(F32)
            own[0][r, a, b] = (gate * jax.nn.sigmoid(gate) * up).astype(BF)
        else:
            gate, up, grad = acts[r, :, low].astype(F32), acts[r, :, high].astype(F32), total(0).astype(F32)
            sig = jax.nn.sigmoid(gate)
            own[1][r, a, b, :, low] = (grad * up * sig * (1.0 + gate * (1.0 - sig))).astype(BF)
            own[1][r, a, b, :, high] = (grad * gate * sig).astype(BF)
        start(unit, "c1", own[g].at[r, a, b], own[g].at[r, a, b], b_next)
        start(unit, "c1", own[g].at[r, a, b], own[g].at[r, a, b], b_prev)
        if unit in FAR_C:
            start(unit, "c2", own[g].at[r, a, b], own[g].at[r, a, b], b_far)

    def stage5(unit):
        r, g = unit
        left, right = AG_LEFT[g], AG_RIGHT[g]
        arrived(unit, "c1", own[g].at[r, a, pl.ds(0, 2)])
        start(unit, "c2", own[g].at[r, a, b3, :, left], own[g].at[r, a, b3, :, left], b_next)
        start(unit, "c2", own[g].at[r, a, b1, :, right], own[g].at[r, a, b1, :, right], b_prev)

    def share(unit, k):
        r, g = unit
        start(unit, "s", own[g].at[r, k], other[g].at[r, :, k], partner)

    def stage6(unit):
        r, g = unit
        if unit in FAR_C:
            arrived(unit, "c1", own[g].at[r, a, pl.ds(0, 2)])
        arrived(unit, "c2", own[g].at[r, a, b2])
        start(unit, "d1", own[g].at[r, a], own[g].at[r, a], a_next)
        start(unit, "d1", own[g].at[r, a], own[g].at[r, a], a_prev)
        if unit in FAR_A:
            start(unit, "d2", own[g].at[r, a], own[g].at[r, a], a_far)
        share(unit, a)

    def stage7(unit):
        r, g = unit
        left, right = AG_LEFT[g], AG_RIGHT[g]
        arrived(unit, "d1", own[g].at[r, pl.ds(0, 2)])
        if unit not in FAR_A:
            start(unit, "d2", own[g].at[r, a3, :, :, left], own[g].at[r, a3, :, :, left], a_next)
            start(unit, "d2", own[g].at[r, a1, :, :, right], own[g].at[r, a1, :, :, right], a_prev)
        share(unit, a1)
        share(unit, a3)

    def stage8(unit):
        r, g = unit
        arrived(unit, "d2", own[g].at[r, a2])
        share(unit, a2)

    def stage9(unit):
        r, g = unit
        arrived(unit, "s", other[g].at[r])
        ours, rest = flat(own[g][r]), flat(other[g][r])
        if g == 0:
            use("theirs_down")
            total = dot(ours, dw[core]) + dot(rest, dw[1 - core])
        else:
            use("theirs_gate", "theirs_up")
            total = dot_t(ours, gu[core]) + dot_t(rest, gu[1 - core])
        z_part[g, r] = total.astype(BF).reshape((RING, RING, ROWS, WIDTH))
        if unit not in TREE:
            for j in (4, 3, 5, 2, 6, 1, 7):
                start(unit, "e1", piece(z_part, unit, j), z_rec.at[g, r, j - 1], others[j - 1])
            return
        start(unit, "e1", piece(z_part, unit, 5), z_rec.at[g, r, 0], others[6])
        start(unit, "e1", piece(z_part, unit, 3), z_rec.at[g, r, 1], others[0])
        start(unit, "e1", piece(z_part, unit, 4).at[0], z_rec.at[g, r, 2, 0], others[5])
        start(unit, "e1", piece(z_part, unit, 4).at[1], z_rec.at[g, r, 2, 1], others[1])
        start(unit, "e2", piece(z_part, unit, 1), z_rec.at[g, r, 3], others[0])
        start(unit, "e2", piece(z_part, unit, 7), z_rec.at[g, r, 4], others[6])

    def piece(ref, unit, by):
        r, g = unit
        target = (z + by) % N_Z
        return ref.at[g, r, target // 2, pl.ds((target % 2) * 2, 2)]

    def stage15(unit):
        r, g = unit
        arrived(unit, "e1", z_rec.at[g, r, pl.ds(0, 3)])
        for by, slot, half in ((6, 0, 0), (2, 1, 1)):
            here = piece(z_part, unit, by)
            total = here[...].astype(F32) + z_rec[g, r, slot].astype(F32)
            both = [total[0], total[1]]
            both[half] = both[half] + z_rec[g, r, 2, half].astype(F32)
            here[0] = both[0].astype(BF)
            here[1] = both[1].astype(BF)
        start(unit, "e2", piece(z_part, unit, 6), z_rec.at[g, r, 5], others[5])
        start(unit, "e2", piece(z_part, unit, 2), z_rec.at[g, r, 6], others[1])

    def stage10(unit):
        r, g = unit
        tree = unit in TREE
        total = piece(z_part, unit, 0)[...].astype(F32)
        if tree:
            arrived(unit, "e2", z_rec.at[g, r, pl.ds(3, 4)])
        else:
            arrived(unit, "e1", z_rec.at[g, r])
        for j in (3, 4, 5, 6) if tree else range(N_Z - 1):
            total = total + z_rec[g, r, j].astype(F32)
        here = piece(z_sum, unit, 0)
        here[...] = total.astype(BF)
        for j in (2, 6, 1, 7) if tree else (4, 3, 5, 2, 6, 1, 7):
            start(unit, "f1" if j in (2, 6) or not tree else "f2", here, here, others[j - 1])

    def stage16(unit):
        r, g = unit
        arrived(unit, "f1", z_rec.at[g, r, pl.ds(0, 2)])
        far = piece(z_sum, unit, 6)
        start(unit, "f2", far, far, others[0])
        start(unit, "f2", far.at[0], far.at[0], others[1])
        far = piece(z_sum, unit, 2)
        start(unit, "f2", far, far, others[6])
        start(unit, "f2", far.at[1], far.at[1], others[5])

    def stage11(unit):
        r, g = unit
        if unit in TREE:
            arrived(unit, "f2", z_rec.at[g, r, pl.ds(0, 5)])
        else:
            arrived(unit, "f1", z_rec.at[g, r])

    def tall(held, cols):
        return held[:, :, :, :, cols].reshape((CHUNKS * BLOCK, cols.size))

    def stage12(unit):
        k = unit[0]
        held = (own, other)[k][0]
        c = cot_t[...]
        for n in range(0, HALF, 256):
            cols = pl.ds(n, min(256, HALF - n))
            grads_d[k, cols, :] = dot(c, tall(held, cols)).T.astype(BF)

    def stage13(unit):
        k = unit[0]
        held = (own, other)[k][1]
        t = tok_t[...]
        for n in range(7):
            cols = pl.ds(n * 256, 256)
            grads[k, :, cols] = dot(t, tall(held, cols)).astype(BF)

    def stage14(unit):
        use("tok0", "tok1", "cot0", "cot1")
        tok_t[...] = tok[...].reshape((CHUNKS * BLOCK, WIDTH)).T
        cot_t[...] = cot[...].reshape((CHUNKS * BLOCK, WIDTH)).T

    stages = [
        stage0, stage1, stage2, stage3, stage4, stage5, stage6, stage7, stage8, stage9, stage10, stage11,
        stage12, stage13, stage14, stage15, stage16,
    ]
    for i, r, g in ORDER:
        stages[i]((r, g))
    for copy in swaps:
        copy.wait_send()

    def all_sent(i, ref):
        remote(ref, ref, send.at[i], recv.at[0, 0], partner).wait_send()

    for g in range(2):
        all_sent(g, z_rec)
        all_sent(2 + g, part[g].at[:, pl.ds(0, 3)])
        all_sent(4 + g, part[g].at[:, 0, pl.ds(0, 3)])
        all_sent(6 + g, own[g].at[:, 0, pl.ds(0, 3)])
        all_sent(8 + g, own[g].at[:, pl.ds(0, 3)])
        all_sent(10 + g, own[g])
    use(*list(waits))


def write_out(z_sum, grads, grads_d, out, tok_grad, gate_grad, up_grad, down_grad, sems):
    core = lax.axis_index("row") % 2
    copies = []

    def copy(src, dst):
        copies.append(pltpu.make_async_copy(src, dst, sems.at[len(copies)]))

    for k, half in enumerate((core, 1 - core)):
        cols = pl.ds(pl.multiple_of(half * HALF, 128), HALF)
        copy(grads.at[k, :, pl.ds(0, HALF)], gate_grad.at[:, cols])
        copy(grads.at[k, :, pl.ds(HALF, HALF)], up_grad.at[:, cols])
        copy(grads_d.at[k], down_grad.at[half])
    for each in copies:
        each.start()
    for g, array in enumerate((out, tok_grad)):
        copy(z_sum.at[g], array)

        @pl.when(core == 0)
        def _():
            copies[-1].start()

        @pl.when(core == 1)
        def _():
            for k in range(4):
                pltpu.make_async_copy(z_sum.at[g, :, k], array.at[:, :, k], sems.at[len(copies) - 1]).start()

    for each in copies:
        each.wait()


def per_device(tokens, gate_weight, up_weight, down_weight, cotangent):
    rows = (CHUNKS, RING, RING, ROWS, WIDTH)
    grad = (CHUNKS, RING, RING, ROWS)
    V = pltpu.VMEM

    def pair(shape, cols):
        return tuple(V(shape + (n,), BF) for n in cols)

    S = jax.ShapeDtypeStruct
    hbm, vmem = pl.BlockSpec(memory_space=pltpu.HBM), pl.BlockSpec(memory_space=pltpu.VMEM)
    results = pl.pallas_call(
        kernel,
        out_shape=(V((2,) + rows, BF), V((2, WIDTH, 2 * HALF), BF), V((2, HALF, WIDTH), BF)),
        in_specs=[hbm] * 5,
        out_specs=[vmem] * 3,
        scratch_shapes=[
            V(rows, BF), V(rows, BF), V(rows, BF), V(rows, BF),
            V((2, WIDTH, 2 * HALF), BF), V((WIDTH, 2 * HALF), BF),
            V((2, HALF, WIDTH), BF), V((HALF, WIDTH), BF),
            V((WIDTH, CHUNKS * BLOCK), BF), V((WIDTH, CHUNKS * BLOCK), BF),
            pair(grad, (2 * HALF, HALF)),
            pair((CHUNKS, RING, ROWS), (2 * HALF, HALF)),
            pair((CHUNKS, 2, RING, ROWS), (2 * HALF, HALF)),
            pair((CHUNKS, RING, ROWS), (2 * HALF, HALF)),
            pair((CHUNKS, ROWS), (2 * HALF, HALF)),
            pair((CHUNKS, 2, ROWS), (2 * HALF, HALF)),
            V((CHUNKS, ROWS, 2 * HALF), BF),
            pair(grad, (HALF, 2 * HALF)), pair(grad, (HALF, 2 * HALF)),
            V((2,) + rows, BF),
            V((2, CHUNKS, N_Z - 1, 2, ROWS, WIDTH), BF),
            pltpu.SemaphoreType.DMA((12,)), pltpu.SemaphoreType.DMA((len(KINDS), 2 * CHUNKS)),
            pltpu.SemaphoreType.DMA((7,)), pltpu.SemaphoreType.DMA((7,)), pltpu.SemaphoreType.DMA((10,)),
        ],
        compiler_params=pltpu.CompilerParams(
            collective_id=0, has_side_effects=True, vmem_limit_bytes=60 << 20
        ),
    )(
        tokens.reshape(rows), gate_weight, up_weight, down_weight.reshape((2, HALF, WIDTH)), cotangent.reshape(rows),
    )
    output, tokens_grad, gate_grad, up_grad, down_grad = pl.pallas_call(
        write_out,
        out_shape=(
            S(rows, BF), S(rows, BF), S((WIDTH, 2 * HALF), BF), S((WIDTH, 2 * HALF), BF), S((2, HALF, WIDTH), BF),
        ),
        in_specs=[vmem] * 3,
        out_specs=[hbm] * 5,
        scratch_shapes=[pltpu.SemaphoreType.DMA((8,))],
        compiler_params=pltpu.CompilerParams(vmem_limit_bytes=1 << 20),
    )(*results)
    return (
        output.reshape(tokens.shape), tokens_grad.reshape(tokens.shape), gate_grad, up_grad,
        down_grad.reshape(down_weight.shape),
    )


def solution(mesh):
    return jax.shard_map(
        per_device,
        mesh=mesh,
        in_specs=(
            P(None, "row"),
            P("row", "col"),
            P("row", "col"),
            P("col", "row"),
            P(None, "row"),
        ),
        out_specs=(
            P(None, "row"),
            P(None, "row"),
            P("row", "col"),
            P("row", "col"),
            P("col", "row"),
        ),
        check_vma=False,
    )
```

```python
import itertools

import jax
import jax.numpy as jnp
from jax import lax
from jax.experimental import pallas as pl
from jax.experimental.pallas import tpu as pltpu
from jax.sharding import PartitionSpec as P

MESH = pl.DeviceIdType.MESH
BF, F32 = jnp.bfloat16, jnp.float32
CHUNKS, RING, ROWS, N_Z = 4, 4, 16, 8
BLOCK = RING * RING * ROWS
WIDTH, HALF = 256, 896
FAR_B, FAR_C, FAR_A = (), (), ()
KINDS = ("a1", "a2", "b1", "b2", "c1", "c2", "d1", "d2", "s", "e1", "e2", "f1", "f2")
SENDS = "efabcds"
TREE = ((0, 0), (0, 1), (1, 0), (1, 1), (2, 0), (2, 1), (3, 0))
Z_PEERS = (1, 2, 3, 4, 5, 6, 7)
RS_LEFT, RS_RIGHT = (pl.ds(0, 896), pl.ds(0, 512)), (pl.ds(896, 896), pl.ds(512, 384))
AG_LEFT, AG_RIGHT = (pl.ds(0, 512), pl.ds(0, 896)), (pl.ds(512, 384), pl.ds(896, 896))

ORDER = [
    (0, 0, 0), (0, 0, 1), (14, 0, 0), (0, 1, 0), (1, 0, 0), (1, 0, 1), (0, 1, 1), (1, 1, 0),
    (0, 2, 0), (2, 0, 0), (2, 0, 1), (1, 1, 1), (2, 1, 0), (0, 2, 1), (1, 2, 0), (3, 0, 0),
    (3, 0, 1), (0, 3, 0), (3, 1, 0), (2, 1, 1), (1, 2, 1), (2, 2, 0), (4, 0, 0), (4, 0, 1),
    (1, 3, 0), (4, 1, 0), (3, 1, 1), (0, 3, 1), (2, 2, 1), (3, 2, 0), (5, 0, 0), (5, 0, 1),
    (2, 3, 0), (5, 1, 0), (4, 1, 1), (1, 3, 1), (3, 2, 1), (4, 2, 0), (6, 0, 0), (6, 0, 1),
    (3, 3, 0), (6, 1, 0), (5, 1, 1), (2, 3, 1), (4, 2, 1), (5, 2, 0), (7, 0, 0), (7, 0, 1),
    (4, 3, 0), (7, 1, 0), (6, 1, 1), (3, 3, 1), (5, 2, 1), (6, 2, 0), (8, 0, 0), (8, 0, 1),
    (9, 0, 0), (5, 3, 0), (8, 1, 0), (9, 0, 1), (9, 1, 0), (7, 1, 1), (4, 3, 1), (15, 0, 0),
    (6, 2, 1), (7, 2, 0), (15, 0, 1), (6, 3, 0), (15, 1, 0), (8, 1, 1), (10, 0, 0), (5, 3, 1),
    (9, 1, 1), (10, 0, 1), (10, 1, 0), (7, 2, 1), (8, 2, 0), (16, 0, 0), (7, 3, 0), (9, 2, 0),
    (6, 3, 1), (15, 1, 1), (16, 0, 1), (8, 2, 1), (16, 1, 0), (8, 3, 0), (9, 2, 1), (11, 0, 0),
    (9, 3, 0), (15, 2, 0), (12, 0, 0), (7, 3, 1), (10, 1, 1), (11, 0, 1), (11, 1, 0), (12, 1, 0),
    (15, 2, 1), (15, 3, 0), (8, 3, 1), (10, 2, 0), (16, 1, 1), (9, 3, 1), (10, 2, 1), (10, 3, 0),
    (16, 2, 0), (11, 1, 1), (10, 3, 1), (16, 2, 1), (16, 3, 0), (13, 1, 1), (13, 0, 1), (11, 2, 0),
    (11, 3, 1), (11, 2, 1), (11, 3, 0),
]


def dot(left, right):
    return jnp.dot(left, right, preferred_element_type=F32)


def dot_t(left, right):
    return lax.dot_general(left, right, (((1,), (1,)), ((), ())), preferred_element_type=F32)


def kernel(
    tok_in, gw_in, uw_in, dw_in, cot_in,
    z_sum, grads, grads_d,
    tok, cot, tok_p, cot_p, gu, gu_p, dw, dw_p, tok_t, cot_t,
    part, rec_in, rec_out, summed, sec_in, sec_out,
    acts, own, other, z_part, z_rec,
    send, recv, swap_send, swap_recv, local,
):
    row, z = lax.axis_index("row"), lax.axis_index("col")
    y, x, core = row // 8, (row // 2) % 4, row % 2
    a = x + core * (y - x)
    b = y + core * (x - y)

    def step_a(by):
        return (
            ((y + core * by + 4) % 4) * 8 + ((x + (1 - core) * by + 4) % 4) * 2 + core,
            z,
        )

    def step_b(by):
        return (
            ((y + (1 - core) * by + 4) % 4) * 8 + ((x + core * by + 4) % 4) * 2 + core,
            z,
        )

    a_next, a_prev, b_next, b_prev = step_a(1), step_a(-1), step_b(1), step_b(-1)
    a_far, b_far = step_a(2), step_b(2)
    partner = (y * 8 + x * 2 + 1 - core, z)
    others = [(row, (z + j) % N_Z) for j in range(1, N_Z)]
    a1, a2, a3 = (a + 1) % 4, (a + 2) % 4, (a + 3) % 4
    b1, b2, b3 = (b + 1) % 4, (b + 2) % 4, (b + 3) % 4
    theirs = pl.multiple_of((1 - core) * HALF, 128)

    waits, counter = {}, itertools.count()

    def rows_of(ref, first, count):
        return ref.at[pl.ds(first, count)]

    def load(name, src, dst):
        copy = pltpu.make_async_copy(src, dst, local.at[next(counter)])
        waits[name] = copy.wait
        copy.start()

    def load_rows(name, src, dst, first, count):
        sem = local.at[next(counter)]
        waits[name] = pltpu.make_async_copy(rows_of(src, first, count), rows_of(dst, first, count), sem).wait

        @pl.when(core == 0)
        def _():
            pltpu.make_async_copy(rows_of(src, first, count), rows_of(dst, first, count), sem).start()

        @pl.when(core == 1)
        def _():
            for k in range(4):
                pltpu.make_async_copy(
                    src.at[pl.ds(first, count), :, k], dst.at[pl.ds(first, count), k], sem
                ).start()

    def use(*names):
        for name in names:
            if name in waits:
                waits.pop(name)()

    def load_weights(name, half):
        cols = pl.ds(pl.multiple_of(half * HALF, 128), HALF)
        load(name + "_gate", gw_in.at[:, cols], gu.at[half, :, pl.ds(0, HALF)])
        load(name + "_up", uw_in.at[:, cols], gu.at[half, :, pl.ds(HALF, HALF)])
        load(name + "_down", dw_in.at[half], dw.at[half])

    load_rows("tok0", tok_in, tok, 0, 1)
    load_weights("mine", core)
    load_rows("cot0", cot_in, cot, 0, 1)

    barrier = pltpu.get_barrier_semaphore()
    peers = [partner, a_next, a_prev, b_next, b_prev] + [a_far] * bool(FAR_A) + [b_far] * bool(FAR_B + FAR_C)
    peers += [others[j - 1] for j in Z_PEERS]
    for peer in peers:
        pl.semaphore_signal(barrier, inc=1, device_id=peer, device_id_type=MESH)
    pl.semaphore_wait(barrier, len(peers))

    def remote(src, dst, s, r, to):
        return pltpu.make_async_remote_copy(
            src_ref=src, dst_ref=dst, send_sem=s, recv_sem=r, device_id=to, device_id_type=MESH
        )

    swaps = []

    def swap(name, src, dst):
        copy = remote(src, dst, swap_send.at[len(swaps)], swap_recv.at[len(swaps)], partner)
        swaps.append(copy)
        waits[name] = copy.wait_recv
        copy.start()

    def swap_rows(name, src, dst, first, count):
        i = len(swaps)

        def part_copy(src, dst):
            return remote(src, dst, swap_send.at[i], swap_recv.at[i], partner)

        whole = part_copy(rows_of(src, first, count), rows_of(dst, first, count))
        swaps.append(whole)
        waits[name] = whole.wait_recv

        @pl.when(core == 1)
        def _():
            whole.start()

        @pl.when(core == 0)
        def _():
            for k in range(4):
                part_copy(src.at[pl.ds(first, count), :, k], dst.at[pl.ds(first, count), k]).start()

    swap_rows("tok_p0", tok_in, tok_p, 0, 1)
    swap("gate_p", gw_in.at[:, pl.ds(theirs, HALF)], gu_p.at[:, pl.ds(0, HALF)])
    swap("up_p", uw_in.at[:, pl.ds(theirs, HALF)], gu_p.at[:, pl.ds(HALF, HALF)])
    swap_rows("cot_p0", cot_in, cot_p, 0, 1)
    swap("down_p", dw_in.at[1 - core], dw_p)
    swap_rows("tok_p1", tok_in, tok_p, 1, CHUNKS - 1)
    swap_rows("cot_p1", cot_in, cot_p, 1, CHUNKS - 1)
    load_rows("tok1", tok_in, tok, 1, CHUNKS - 1)
    load_rows("cot1", cot_in, cot, 1, CHUNKS - 1)
    load_weights("theirs", 1 - core)

    def start(unit, kind, src, dst, to):
        r, g = unit
        place = SENDS.index(kind[0])
        out_sem = place if place < 2 else 2 * place - 2 + g
        remote(src, dst, send.at[out_sem], recv.at[KINDS.index(kind), 2 * r + g], to).start()

    def arrived(unit, kind, ref):
        r, g = unit
        remote(ref, ref, send.at[0], recv.at[KINDS.index(kind), 2 * r + g], partner).wait_recv()

    def flat(value):
        return value.reshape((BLOCK, value.shape[-1]))

    def add(blocks, begin, size, into, *terms):
        width = min(size, HALF)

        def step(i, carry):
            for n in range(begin, begin + size, width):
                total = terms[0](i, n, width).astype(F32)
                for term in terms[1:]:
                    total = total + term(i, n, width).astype(F32)
                into(i, n, width, total.astype(BF))
            return carry

        lax.fori_loop(0, blocks, step, 0)

    def stage0(unit):
        r, g = unit
        late = "" if r == 0 else "1"
        dst = part[g]
        if g == 0:
            use("tok0", "tok_p0", "tok" + late, "tok_p" + late)
            mine, theirs = flat(tok[r]), flat(tok_p[r])
        else:
            use("cot0", "mine_down", "cot_p0", "down_p", "cot" + late, "cot_p" + late)
            mine, theirs = flat(cot[r]), flat(cot_p[r])

        def project(side):
            for n in range(side.start, side.start + side.size, 256):
                size = min(256, side.start + side.size - n)
                cols = pl.ds(n, size)
                if g == 0:
                    total = dot(mine, gu[core, :, cols]) + dot(theirs, gu_p[:, cols])
                else:
                    total = dot_t(mine, dw[core, cols, :]) + dot_t(theirs, dw_p[cols, :])
                dst[r, :, :, :, cols] = total.astype(BF).reshape((RING, RING, ROWS, size))

        left, right = RS_LEFT[g], RS_RIGHT[g]
        if g == 0:
            use("mine_gate", "gate_p")
        project(left)
        start(unit, "a1", dst.at[r, a2, :, :, left], rec_in[g].at[r, :, :, left], a_next)
        if g == 0:
            use("mine_up", "up_p")
        project(right)
        start(unit, "a1", dst.at[r, a2, :, :, right], rec_in[g].at[r, :, :, right], a_prev)
        start(unit, "a2", dst.at[r, a1, :, :, right], rec_out[g].at[r, 0, :, :, right], a_next)
        start(unit, "a2", dst.at[r, a3, :, :, left], rec_out[g].at[r, 1, :, :, left], a_prev)

    def stage1(unit):
        r, g = unit
        left, right = RS_LEFT[g], RS_RIGHT[g]
        ref, held = part[g], rec_in[g]
        arrived(unit, "a1", held.at[r])

        def put_left(i, n, width, value):
            ref[r, a1, i, :, pl.ds(n, width)] = value

        add(
            4, 0, left.size, put_left,
            lambda i, n, width: ref[r, a1, i, :, pl.ds(n, width)],
            lambda i, n, width: held[r, i, :, pl.ds(n, width)],
        )
        start(unit, "a2", ref.at[r, a1, :, :, left], rec_out[g].at[r, 0, :, :, left], a_next)

        def put_right(i, n, width, value):
            ref[r, a3, i, :, pl.ds(n, width)] = value

        add(
            4, right.start, right.size, put_right,
            lambda i, n, width: ref[r, a3, i, :, pl.ds(n, width)],
            lambda i, n, width: held[r, i, :, pl.ds(n, width)],
        )
        start(unit, "a2", ref.at[r, a3, :, :, right], rec_out[g].at[r, 1, :, :, right], a_prev)

    def stage2(unit):
        r, g = unit
        left, right = RS_LEFT[g], RS_RIGHT[g]
        ref, held, to = part[g], rec_out[g], summed[g]
        arrived(unit, "a2", held.at[r])

        def put(i, n, width, value):
            to[r, i, :, pl.ds(n, width)] = value

        add(
            4, 0, left.size + right.size, put,
            lambda i, n, width: ref[r, a, i, :, pl.ds(n, width)],
            lambda i, n, width: held[r, 0, i, :, pl.ds(n, width)],
            lambda i, n, width: held[r, 1, i, :, pl.ds(n, width)],
        )
        if unit in FAR_B:
            start(unit, "b1", to.at[r, b2], sec_in[g].at[r], b_far)
            start(unit, "b2", to.at[r, b1], sec_out[g].at[r, 0], b_next)
            start(unit, "b2", to.at[r, b3], sec_out[g].at[r, 1], b_prev)
            return
        start(unit, "b1", to.at[r, b2, :, left], sec_in[g].at[r, :, left], b_next)
        start(unit, "b1", to.at[r, b2, :, right], sec_in[g].at[r, :, right], b_prev)
        start(unit, "b2", to.at[r, b1, :, right], sec_out[g].at[r, 0, :, right], b_next)
        start(unit, "b2", to.at[r, b3, :, left], sec_out[g].at[r, 1, :, left], b_prev)

    def stage3(unit):
        r, g = unit
        left, right = RS_LEFT[g], RS_RIGHT[g]
        ref = summed[g]
        arrived(unit, "b1", sec_in[g].at[r])
        value = ref[r, b1, :, left].astype(F32) + sec_in[g][r, :, left].astype(F32)
        ref[r, b1, :, left] = value.astype(BF)
        start(unit, "b2", ref.at[r, b1, :, left], sec_out[g].at[r, 0, :, left], b_next)
        value = ref[r, b3, :, right].astype(F32) + sec_in[g][r, :, right].astype(F32)
        ref[r, b3, :, right] = value.astype(BF)
        start(unit, "b2", ref.at[r, b3, :, right], sec_out[g].at[r, 1, :, right], b_prev)

    def stage4(unit):
        r, g = unit
        if unit in FAR_B:
            arrived(unit, "b1", sec_in[g].at[r])
        arrived(unit, "b2", sec_out[g].at[r])

        def total(k):
            cols = pl.ds(k * HALF, HALF)
            value = summed[g][r, b, :, cols].astype(F32) + sec_out[g][r, 0, :, cols].astype(F32)
            value = value + sec_out[g][r, 1, :, cols].astype(F32)
            if unit in FAR_B:
                value = value + sec_in[g][r, :, cols].astype(F32)
            return value.astype(BF)

        low, high = pl.ds(0, HALF), pl.ds(HALF, HALF)
        if g == 0:
            gate_bf, up_bf = total(0), total(1)
            acts[r, :, low] = gate_bf
            acts[r, :, high] = up_bf
            gate, up = gate_bf.astype(F32), up_bf.astype(F32)
            own[0][r, a, b] = (gate * jax.nn.sigmoid(gate) * up).astype(BF)
        else:
            gate, up, grad = acts[r, :, low].astype(F32), acts[r, :, high].astype(F32), total(0).astype(F32)
            sig = jax.nn.sigmoid(gate)
            own[1][r, a, b, :, low] = (grad * up * sig * (1.0 + gate * (1.0 - sig))).astype(BF)
            own[1][r, a, b, :, high] = (grad * gate * sig).astype(BF)
        start(unit, "c1", own[g].at[r, a, b], own[g].at[r, a, b], b_next)
        start(unit, "c1", own[g].at[r, a, b], own[g].at[r, a, b], b_prev)
        if unit in FAR_C:
            start(unit, "c2", own[g].at[r, a, b], own[g].at[r, a, b], b_far)

    def stage5(unit):
        r, g = unit
        left, right = AG_LEFT[g], AG_RIGHT[g]
        arrived(unit, "c1", own[g].at[r, a, pl.ds(0, 2)])
        start(unit, "c2", own[g].at[r, a, b3, :, left], own[g].at[r, a, b3, :, left], b_next)
        start(unit, "c2", own[g].at[r, a, b1, :, right], own[g].at[r, a, b1, :, right], b_prev)

    def share(unit, k):
        r, g = unit
        start(unit, "s", own[g].at[r, k], other[g].at[r, :, k], partner)

    def stage6(unit):
        r, g = unit
        if unit in FAR_C:
            arrived(unit, "c1", own[g].at[r, a, pl.ds(0, 2)])
        arrived(unit, "c2", own[g].at[r, a, b2])
        start(unit, "d1", own[g].at[r, a], own[g].at[r, a], a_next)
        start(unit, "d1", own[g].at[r, a], own[g].at[r, a], a_prev)
        if unit in FAR_A:
            start(unit, "d2", own[g].at[r, a], own[g].at[r, a], a_far)
        share(unit, a)

    def stage7(unit):
        r, g = unit
        left, right = AG_LEFT[g], AG_RIGHT[g]
        arrived(unit, "d1", own[g].at[r, pl.ds(0, 2)])
        if unit not in FAR_A:
            start(unit, "d2", own[g].at[r, a3, :, :, left], own[g].at[r, a3, :, :, left], a_next)
            start(unit, "d2", own[g].at[r, a1, :, :, right], own[g].at[r, a1, :, :, right], a_prev)
        share(unit, a1)
        share(unit, a3)

    def stage8(unit):
        r, g = unit
        arrived(unit, "d2", own[g].at[r, a2])
        share(unit, a2)

    def stage9(unit):
        r, g = unit
        arrived(unit, "s", other[g].at[r])
        ours, rest = flat(own[g][r]), flat(other[g][r])
        if g == 0:
            use("theirs_down")
            total = dot(ours, dw[core]) + dot(rest, dw[1 - core])
        else:
            use("theirs_gate", "theirs_up")
            total = dot_t(ours, gu[core]) + dot_t(rest, gu[1 - core])
        z_part[g, r] = total.astype(BF).reshape((RING, RING, ROWS, WIDTH))
        if unit not in TREE:
            for j in (4, 3, 5, 2, 6, 1, 7):
                start(unit, "e1", piece(z_part, unit, j), z_rec.at[g, r, j - 1], others[j - 1])
            return
        start(unit, "e1", piece(z_part, unit, 5), z_rec.at[g, r, 0], others[6])
        start(unit, "e1", piece(z_part, unit, 3), z_rec.at[g, r, 1], others[0])
        start(unit, "e1", piece(z_part, unit, 4).at[0], z_rec.at[g, r, 2, 0], others[5])
        start(unit, "e1", piece(z_part, unit, 4).at[1], z_rec.at[g, r, 2, 1], others[1])
        start(unit, "e2", piece(z_part, unit, 1), z_rec.at[g, r, 3], others[0])
        start(unit, "e2", piece(z_part, unit, 7), z_rec.at[g, r, 4], others[6])

    def piece(ref, unit, by):
        r, g = unit
        target = (z + by) % N_Z
        return ref.at[g, r, target // 2, pl.ds((target % 2) * 2, 2)]

    def stage15(unit):
        r, g = unit
        arrived(unit, "e1", z_rec.at[g, r, pl.ds(0, 3)])
        for by, slot, half in ((6, 0, 0), (2, 1, 1)):
            here = piece(z_part, unit, by)
            total = here[...].astype(F32) + z_rec[g, r, slot].astype(F32)
            both = [total[0], total[1]]
            both[half] = both[half] + z_rec[g, r, 2, half].astype(F32)
            here[0] = both[0].astype(BF)
            here[1] = both[1].astype(BF)
        start(unit, "e2", piece(z_part, unit, 6), z_rec.at[g, r, 5], others[5])
        start(unit, "e2", piece(z_part, unit, 2), z_rec.at[g, r, 6], others[1])

    def stage10(unit):
        r, g = unit
        tree = unit in TREE
        total = piece(z_part, unit, 0)[...].astype(F32)
        if tree:
            arrived(unit, "e2", z_rec.at[g, r, pl.ds(3, 4)])
        else:
            arrived(unit, "e1", z_rec.at[g, r])
        for j in (3, 4, 5, 6) if tree else range(N_Z - 1):
            total = total + z_rec[g, r, j].astype(F32)
        here = piece(z_sum, unit, 0)
        here[...] = total.astype(BF)
        for j in (2, 6, 1, 7) if tree else (4, 3, 5, 2, 6, 1, 7):
            start(unit, "f1" if j in (2, 6) or not tree else "f2", here, here, others[j - 1])

    def stage16(unit):
        r, g = unit
        arrived(unit, "f1", z_rec.at[g, r, pl.ds(0, 2)])
        far = piece(z_sum, unit, 6)
        start(unit, "f2", far, far, others[0])
        start(unit, "f2", far.at[0], far.at[0], others[1])
        far = piece(z_sum, unit, 2)
        start(unit, "f2", far, far, others[6])
        start(unit, "f2", far.at[1], far.at[1], others[5])

    def stage11(unit):
        r, g = unit
        if unit in TREE:
            arrived(unit, "f2", z_rec.at[g, r, pl.ds(0, 5)])
        else:
            arrived(unit, "f1", z_rec.at[g, r])

    def tall(held, cols):
        return held[:, :, :, :, cols].reshape((CHUNKS * BLOCK, cols.size))

    def stage12(unit):
        k = unit[0]
        held = (own, other)[k][0]
        c = cot_t[...]
        for n in range(0, HALF, 256):
            cols = pl.ds(n, min(256, HALF - n))
            grads_d[k, cols, :] = dot(c, tall(held, cols)).T.astype(BF)

    def stage13(unit):
        k = unit[0]
        held = (own, other)[k][1]
        t = tok_t[...]
        for n in range(7):
            cols = pl.ds(n * 256, 256)
            grads[k, :, cols] = dot(t, tall(held, cols)).astype(BF)

    def stage14(unit):
        use("tok0", "tok1", "cot0", "cot1")
        tok_t[...] = tok[...].reshape((CHUNKS * BLOCK, WIDTH)).T
        cot_t[...] = cot[...].reshape((CHUNKS * BLOCK, WIDTH)).T

    stages = [
        stage0, stage1, stage2, stage3, stage4, stage5, stage6, stage7, stage8, stage9, stage10, stage11,
        stage12, stage13, stage14, stage15, stage16,
    ]
    for i, r, g in ORDER:
        stages[i]((r, g))
    for copy in swaps:
        copy.wait_send()

    def all_sent(i, ref):
        remote(ref, ref, send.at[i], recv.at[0, 0], partner).wait_send()

    for g in range(2):
        all_sent(g, z_rec)
        all_sent(2 + g, part[g].at[:, pl.ds(0, 3)])
        all_sent(4 + g, part[g].at[:, 0, pl.ds(0, 3)])
        all_sent(6 + g, own[g].at[:, 0, pl.ds(0, 3)])
        all_sent(8 + g, own[g].at[:, pl.ds(0, 3)])
        all_sent(10 + g, own[g])
    use(*list(waits))


def write_out(z_sum, grads, grads_d, out, tok_grad, gate_grad, up_grad, down_grad, sems):
    core = lax.axis_index("row") % 2
    copies = []

    def copy(src, dst):
        copies.append(pltpu.make_async_copy(src, dst, sems.at[len(copies)]))

    for k, half in enumerate((core, 1 - core)):
        cols = pl.ds(pl.multiple_of(half * HALF, 128), HALF)
        copy(grads.at[k, :, pl.ds(0, HALF)], gate_grad.at[:, cols])
        copy(grads.at[k, :, pl.ds(HALF, HALF)], up_grad.at[:, cols])
        copy(grads_d.at[k], down_grad.at[half])
    for each in copies:
        each.start()
    for g, array in enumerate((out, tok_grad)):
        copy(z_sum.at[g], array)

        @pl.when(core == 0)
        def _():
            copies[-1].start()

        @pl.when(core == 1)
        def _():
            for k in range(4):
                pltpu.make_async_copy(z_sum.at[g, :, k], array.at[:, :, k], sems.at[len(copies) - 1]).start()

    for each in copies:
        each.wait()


def per_device(tokens, gate_weight, up_weight, down_weight, cotangent):
    rows = (CHUNKS, RING, RING, ROWS, WIDTH)
    grad = (CHUNKS, RING, RING, ROWS)
    V = pltpu.VMEM

    def pair(shape, cols):
        return tuple(V(shape + (n,), BF) for n in cols)

    S = jax.ShapeDtypeStruct
    hbm, vmem = pl.BlockSpec(memory_space=pltpu.HBM), pl.BlockSpec(memory_space=pltpu.VMEM)
    results = pl.pallas_call(
        kernel,
        out_shape=(V((2,) + rows, BF), V((2, WIDTH, 2 * HALF), BF), V((2, HALF, WIDTH), BF)),
        in_specs=[hbm] * 5,
        out_specs=[vmem] * 3,
        scratch_shapes=[
            V(rows, BF), V(rows, BF), V(rows, BF), V(rows, BF),
            V((2, WIDTH, 2 * HALF), BF), V((WIDTH, 2 * HALF), BF),
            V((2, HALF, WIDTH), BF), V((HALF, WIDTH), BF),
            V((WIDTH, CHUNKS * BLOCK), BF), V((WIDTH, CHUNKS * BLOCK), BF),
            pair(grad, (2 * HALF, HALF)),
            pair((CHUNKS, RING, ROWS), (2 * HALF, HALF)),
            pair((CHUNKS, 2, RING, ROWS), (2 * HALF, HALF)),
            pair((CHUNKS, RING, ROWS), (2 * HALF, HALF)),
            pair((CHUNKS, ROWS), (2 * HALF, HALF)),
            pair((CHUNKS, 2, ROWS), (2 * HALF, HALF)),
            V((CHUNKS, ROWS, 2 * HALF), BF),
            pair(grad, (HALF, 2 * HALF)), pair(grad, (HALF, 2 * HALF)),
            V((2,) + rows, BF),
            V((2, CHUNKS, N_Z - 1, 2, ROWS, WIDTH), BF),
            pltpu.SemaphoreType.DMA((12,)), pltpu.SemaphoreType.DMA((len(KINDS), 2 * CHUNKS)),
            pltpu.SemaphoreType.DMA((7,)), pltpu.SemaphoreType.DMA((7,)), pltpu.SemaphoreType.DMA((10,)),
        ],
        compiler_params=pltpu.CompilerParams(
            collective_id=0, has_side_effects=True, vmem_limit_bytes=60 << 20
        ),
    )(
        tokens.reshape(rows), gate_weight, up_weight, down_weight.reshape((2, HALF, WIDTH)), cotangent.reshape(rows),
    )
    output, tokens_grad, gate_grad, up_grad, down_grad = pl.pallas_call(
        write_out,
        out_shape=(
            S(rows, BF), S(rows, BF), S((WIDTH, 2 * HALF), BF), S((WIDTH, 2 * HALF), BF), S((2, HALF, WIDTH), BF),
        ),
        in_specs=[vmem] * 3,
        out_specs=[hbm] * 5,
        scratch_shapes=[pltpu.SemaphoreType.DMA((8,))],
        compiler_params=pltpu.CompilerParams(vmem_limit_bytes=1 << 20),
    )(*results)
    return (
        output.reshape(tokens.shape), tokens_grad.reshape(tokens.shape), gate_grad, up_grad,
        down_grad.reshape(down_weight.shape),
    )


def solution(mesh):
    return jax.shard_map(
        per_device,
        mesh=mesh,
        in_specs=(
            P(None, "row"),
            P("row", "col"),
            P("row", "col"),
            P("col", "row"),
            P(None, "row"),
        ),
        out_specs=(
            P(None, "row"),
            P(None, "row"),
            P("row", "col"),
            P("row", "col"),
            P("col", "row"),
        ),
        check_vma=False,
    )
```
